256 devices in a mesh: ctx: 64 (over z, y, core), dp: 4 (over x).
Axes of the slice: x: 4, y: 4, z: 8, core: 2. Of those that a mesh axis runs over, the one named last changes fastest.
Arguments:
- queries: bfloat16 [32768, 1024], P(('dp', 'ctx')), parts along dimension 0, may hold values from -220 to 220
- keys: bfloat16 [32768, 1024], P(('dp', 'ctx')), parts along dimension 0, may hold values from -8 to 8
- values: bfloat16 [32768, 1024], P(('dp', 'ctx')), parts along dimension 0, may hold values from -6 to 6
- cotangent: bfloat16 [32768, 1024], P(('dp', 'ctx')), parts along dimension 0, may hold values from -6 to 6
Outputs:
- output: bfloat16 [32768, 1024], P(('dp', 'ctx')), parts along dimension 0
- grad_queries: bfloat16 [32768, 1024], P(('dp', 'ctx')), parts along dimension 0
- grad_keys: bfloat16 [32768, 1024], P(('dp', 'ctx')), parts along dimension 0
- grad_values: bfloat16 [32768, 1024], P(('dp', 'ctx')), parts along dimension 0
The draws below stay inside these ranges and needn't reach their ends.
There are 4 independent parts, one for each index of `dp`. The reference program is written for one: setup_inputs(seed, part) draws one part's arguments, and reference() takes and returns one part's arrays. A program takes and returns all parts, laid end to end along the dimension named above; each array names one. Nothing has to cross between parts.
All inputs are finite; a program needn't handle non-finite values.
Results may differ from the reference program's by a relative error of at most 0.012.
Values may be sent and summed in bfloat16 or wider, within the bound.
No kernel may reach another device: no remote copies, remote signals or barrier semaphores. Data moves between devices by JAX's collectives and lax.ppermute only.
A program may use at most 128 MiB of HBM per device.

```python
import jax
import jax.numpy as jnp
from jax import lax

D = 1024
H = 8
DH = 128
B = 64
LEVELS = 7
TOKENS = 8192


def key_rows(key):
    base = jnp.clip(jax.random.normal(key, (TOKENS, D), jnp.float32), -4.0, 4.0)
    return base


def draw_keys(key, part):
    shared = key_rows(key)
    return shared.astype(jnp.bfloat16)


def draw_queries(key, part):
    key = jax.random.fold_in(key, 7)
    result = jnp.clip(2.0 * jax.random.normal(key, (TOKENS, D), jnp.float32), -12.0, 12.0)
    return result.astype(jnp.bfloat16)


def levels(rng, extent, cuts, smallest, high):
    gain = 1.0
    for axis_at, blocks in cuts:
        draws = jax.random.uniform(jax.random.fold_in(jax.random.fold_in(rng, 6), axis_at), (blocks,), jnp.float32, smallest / len(cuts), high / len(cuts))
        gain = gain * jnp.repeat(jnp.exp(draws), extent[axis_at] // blocks).reshape((-1,) + (1,) * (len(extent) - 1 - axis_at))
    return gain


def centred(key, dims, scale, most, pieces=(), dtype=jnp.bfloat16):
    drawn = jax.random.normal(key, dims, jnp.float32) * scale
    if len(pieces) > 0:
        drawn = levels(key, dims, pieces, -0.22, 0.18) * drawn
    return jnp.clip(drawn, min=-most, max=most).astype(dtype)


def setup_inputs(seed: int = 0, part: int = 0) -> dict:
    arg_keys = jax.random.split(jax.random.key(seed), 5)
    own_keys = jax.random.split(jax.random.fold_in(arg_keys[4], part), 5)
    return {
        "queries": draw_queries(jax.random.fold_in(jax.random.fold_in(arg_keys[4], part), 71), part),
        "keys": draw_keys(jax.random.fold_in(jax.random.fold_in(arg_keys[4], part), 71), part),
        "values": centred(own_keys[2], (TOKENS, D), 1.0, 6.0, ((0, 64),)),
        "cotangent": centred(own_keys[3], (TOKENS, D), 1.0, 6.0, ((0, 64),)),
    }


half_root = 0.7071067811865476


def coarsen(block_rows):
    total = block_rows.reshape(block_rows.shape[0] // 2, 2, block_rows.shape[1]).astype(jnp.float32).sum(axis=1)
    return (total * half_root).astype(jnp.bfloat16)


def spread(gradient):
    return jnp.repeat(gradient, 2, axis=0) * half_root


def partner(blocks):
    pair_count = blocks.shape[0] // 2
    paired = blocks.reshape((pair_count, 2) + blocks.shape[1:])
    return jnp.flip(paired, axis=1).reshape(blocks.shape)


def head_pass(operands):
    head_query, head_key, head_value, head_grad = operands
    score_scale = DH ** -0.5
    coarse_keys = [head_key]
    coarse_values = [head_value]
    for height in range(1, LEVELS):
        coarse_keys.append(coarsen(coarse_keys[-1]))
        coarse_values.append(coarsen(coarse_values[-1]))
    groups = [(head_key.reshape(TOKENS // B, B, DH).astype(jnp.float32), head_value.reshape(TOKENS // B, B, DH).astype(jnp.float32), B)]
    for height in range(LEVELS):
        group_span = B * 2 ** height
        groups.append((partner(coarse_keys[height].reshape(TOKENS // group_span, B, DH)).astype(jnp.float32),
                       partner(coarse_values[height].reshape(TOKENS // group_span, B, DH)).astype(jnp.float32), group_span))
    query_f = head_query.astype(jnp.float32)
    grad_f = head_grad.astype(jnp.float32)
    scores = jnp.concatenate([jnp.einsum("ngd,nkd->ngk", query_f.reshape(-1, group_span, DH), key_block).reshape(TOKENS, B)
                              for key_block, value_block, group_span in groups], axis=1) * score_scale
    row_top = jnp.max(scores, axis=1, keepdims=True)
    exponent = jnp.exp(scores - row_top)
    probabilities = exponent / jnp.sum(exponent, axis=1, keepdims=True)
    weights = probabilities.astype(jnp.bfloat16)
    dprob = jnp.concatenate([jnp.einsum("ngd,nkd->ngk", grad_f.reshape(-1, group_span, DH), value_block).reshape(TOKENS, B)
                             for key_block, value_block, group_span in groups], axis=1)
    row_delta = jnp.sum(probabilities * dprob, axis=1, keepdims=True)
    dscore = (probabilities * (dprob - row_delta) * score_scale).astype(jnp.bfloat16)
    output = jnp.zeros((TOKENS, DH), jnp.float32)
    grad_query = jnp.zeros((TOKENS, DH), jnp.float32)
    key_parts = []
    value_parts = []
    for number, (key_block, value_block, group_span) in enumerate(groups):
        part_weights = weights[:, number * B:(number + 1) * B].astype(jnp.float32).reshape(-1, group_span, B)
        part_scores = dscore[:, number * B:(number + 1) * B].astype(jnp.float32).reshape(-1, group_span, B)
        output = output + jnp.einsum("ngk,nkd->ngd", part_weights, value_block).reshape(TOKENS, DH)
        grad_query = grad_query + jnp.einsum("ngk,nkd->ngd", part_scores, key_block).reshape(TOKENS, DH)
        key_parts.append(jnp.einsum("ngk,ngd->nkd", part_scores, query_f.reshape(-1, group_span, DH)))
        value_parts.append(jnp.einsum("ngk,ngd->nkd", part_weights, grad_f.reshape(-1, group_span, DH)))
    total_keys = partner(key_parts[LEVELS]).reshape(TOKENS >> (LEVELS - 1), DH)
    total_values = partner(value_parts[LEVELS]).reshape(TOKENS >> (LEVELS - 1), DH)
    for height in reversed(range(LEVELS - 1)):
        total_keys = partner(key_parts[height + 1]).reshape(TOKENS >> height, DH) + spread(total_keys)
        total_values = partner(value_parts[height + 1]).reshape(TOKENS >> height, DH) + spread(total_values)
    grad_key = (total_keys + key_parts[0].reshape(TOKENS, DH)).astype(jnp.bfloat16)
    grad_value = (total_values + value_parts[0].reshape(TOKENS, DH)).astype(jnp.bfloat16)
    return (output.astype(jnp.bfloat16), grad_query.astype(jnp.bfloat16), grad_key, grad_value)


def split_heads(tensor):
    return tensor.reshape(TOKENS, H, DH).transpose(1, 0, 2)


def merge_heads(tensor):
    return tensor.transpose(1, 0, 2).reshape(TOKENS, D)


def reference(queries, keys, values, cotangent):
    results = lax.map(head_pass, (split_heads(queries), split_heads(keys), split_heads(values), split_heads(cotangent)))
    return (merge_heads(results[0]), merge_heads(results[1]), merge_heads(results[2]), merge_heads(results[3]))
```

```python
import jax
import jax.numpy as jnp
from jax import lax
from jax.experimental import pallas as pl
from jax.experimental.pallas import tpu as pltpu
from jax.sharding import PartitionSpec as P

H = 8
DH = 128
D = H * DH
ROWS = 128
Z = 8
HALF_ROOT = 0.7071067811865476
SCALE = DH ** (-0.5)
LOG2E = 1.4426950408889634
F32 = jnp.float32
BF16 = jnp.bfloat16
VMEM_LIMIT = 48 * 1024 * 1024
PARAMS = pltpu.CompilerParams(vmem_limit_bytes=VMEM_LIMIT)


def z_index():
    return lax.axis_index("ctx") // 8


def swap(block, mask):
    count = lax.axis_size("ctx")
    return lax.ppermute(block, "ctx", [(i, i ^ mask) for i in range(count)])


def z_exchange(block):
    groups = [[z * 8 + rest for z in range(Z)] for rest in range(8)]
    return lax.all_to_all(block, "ctx", 0, 0, tiled=True, axis_index_groups=groups)


def place_of(other):
    level = 4 if other == 1 else 5 if other < 4 else 6
    start = 0 if other == 1 else 4 * (other - 2) if other < 4 else 2 * (other - 4)
    return level, start


def coarsen_kernel(k_ref, v_ref, c1_ref, c2_ref, c3_ref, send_ref, tmp, pack):
    z = z_index()
    pack[...] = jnp.zeros(pack.shape, F32)
    for side, source in enumerate((k_ref, v_ref)):
        for number in range(H):
            columns = slice(number * DH, number * DH + DH)
            plane = tmp.at[side * H + number]
            rows = source[:, columns].astype(F32)
            for level in range(1, 7):
                count = ROWS >> level
                plane[: 2 * count, :] = rows
                total = plane[pl.ds(0, count, stride=2), :] + plane[pl.ds(1, count, stride=2), :]
                exact = (total * HALF_ROOT).astype(BF16)
                rows = exact.astype(F32)
                if level < 4:
                    ref = (c1_ref, c2_ref, c3_ref)[level - 1]
                    ref[side * count : side * count + count, columns] = exact
                for other in range(1, Z):
                    at, start = place_of(other)
                    if at == level:
                        start += 16 * other + 8 * side
                        pack[start : start + count, columns] = rows
    for other in range(Z):
        send_ref[z ^ other] = pack[16 * other : 16 * other + 16, :].astype(BF16)


def coarsen(keys, values):
    return pl.pallas_call(
        coarsen_kernel,
        out_shape=(
            jax.ShapeDtypeStruct((128, D), BF16),
            jax.ShapeDtypeStruct((64, D), BF16),
            jax.ShapeDtypeStruct((32, D), BF16),
            jax.ShapeDtypeStruct((Z, 16, D), BF16),
        ),
        scratch_shapes=[pltpu.VMEM((2 * H, ROWS, DH), F32), pltpu.VMEM((16 * Z, D), F32)],
        compiler_params=PARAMS,
        name="coarsen",
    )(keys, values)


def merge_kernel(got_ref, c2_ref, c3_ref, near_ref, far_ref):
    z = z_index()
    tile_a = got_ref[z ^ 1]
    tile_b = got_ref[z ^ 2] + got_ref[z ^ 3]
    tile_c = (got_ref[z ^ 4] + got_ref[z ^ 5]) + (got_ref[z ^ 6] + got_ref[z ^ 7])
    for ref in (near_ref, far_ref):
        ref[0:16, :] = tile_a
        ref[16:32, :] = tile_b
        ref[32:48, :] = tile_c
    near_ref[48:112, :] = c2_ref[...]
    far_ref[48:80, :] = c3_ref[...]


def merge(got, c2, c3):
    return pl.pallas_call(
        merge_kernel,
        out_shape=(
            jax.ShapeDtypeStruct((112, D), BF16),
            jax.ShapeDtypeStruct((80, D), BF16),
        ),
        compiler_params=PARAMS,
        name="merge",
    )(got, c2, c3)


def place(mine, other, c1_ref, key_all, value_all, key_tmp, value_tmp):
    key_all[128:192, :] = c1_ref[0:64, :]
    value_all[128:192, :] = c1_ref[64:128, :]
    for core, refs in enumerate((mine, other)):
        near, far2, far3, own = refs
        start = 192 + 32 * core
        key_all[start : start + 32, :] = near[48:80, :]
        value_all[start : start + 32, :] = near[80:112, :]
        for number, ref in enumerate((far2, far3)):
            start = 256 + 32 * core + 16 * number
            key_all[start : start + 16, :] = ref[48:64, :]
            value_all[start : start + 16, :] = ref[64:80, :]
        for number, ref in enumerate((own, near, far2, far3)):
            for tile in range(3):
                rows = ref[16 * tile : 16 * tile + 16, :].astype(F32)
                start = 96 * core + 24 * number + 8 * tile
                key_tmp[start : start + 8, :] = rows[:8]
                value_tmp[start : start + 8, :] = rows[8:]
    key_all[320:512, :] = key_tmp[...].astype(BF16)
    value_all[320:512, :] = value_tmp[...].astype(BF16)


def collect(key_grad, value_grad, core, out_ref):
    out = 0

    def tiles(number):
        for tile in range(3):
            start = 320 + 96 * core + 24 * number + 8 * tile
            yield key_grad[start : start + 8, :], value_grad[start : start + 8, :]

    def level2():
        start = 192 + 32 * core
        yield key_grad[start : start + 32, :], value_grad[start : start + 32, :]

    def level3(number):
        start = 256 + 32 * core + 16 * number
        yield key_grad[start : start + 16, :], value_grad[start : start + 16, :]

    order = (tiles(1), level2(), tiles(2), level3(0), tiles(3), level3(1), tiles(0))
    for pieces in order:
        for key_piece, value_piece in pieces:
            count = key_piece.shape[0]
            both = jnp.concatenate([key_piece, value_piece], axis=0)
            out_ref[out : out + 2 * count, :] = both.astype(out_ref.dtype)
            out += 2 * count


def attend_kernel(
    q_ref, k_ref, v_ref, g_ref, c1_ref,
    near_ref, far2_ref, far3_ref, own_ref,
    near_o_ref, far2_o_ref, far3_o_ref, own_o_ref,
    out_ref, grad_q_ref, local_k_ref, local_v_ref, one_ref, mine_ref, other_ref,
    key_all, value_all, key_grad, value_grad, key_tmp, value_tmp,
):
    key_all[0:128, :] = k_ref[...]
    value_all[0:128, :] = v_ref[...]
    place(
        (near_ref, far2_ref, far3_ref, own_ref),
        (near_o_ref, far2_o_ref, far3_o_ref, own_o_ref),
        c1_ref, key_all, value_all, key_tmp, value_tmp,
    )

    def dot(a, b, a_dim, b_dim):
        return lax.dot_general(
            a, b, (((a_dim,), (b_dim,)), ((), ())), preferred_element_type=F32
        )

    def head(number, carry):
        columns = pl.ds(pl.multiple_of(number * DH, DH), DH)
        q = q_ref[:, columns]
        g = g_ref[:, columns]
        k = key_all[:, columns]
        v = value_all[:, columns]
        scores = dot(k, q, 1, 1)
        top = jnp.max(scores, axis=0, keepdims=True)
        exponent = jnp.exp2((scores - top) * (SCALE * LOG2E))
        prob = exponent * (1.0 / jnp.sum(exponent, axis=0, keepdims=True))
        weights = prob.astype(BF16)
        dprob = dot(v, g, 1, 1)
        delta = jnp.sum(prob * dprob, axis=0, keepdims=True)
        dscore = (prob * (dprob - delta) * SCALE).astype(BF16)
        out_ref[:, columns] = dot(weights, v, 0, 0).astype(BF16)
        grad_q_ref[:, columns] = dot(dscore, k, 0, 0).astype(BF16)
        key_grad[:, columns] = dot(dscore, q, 1, 0)
        value_grad[:, columns] = dot(weights, g, 1, 0)
        return carry

    lax.fori_loop(0, H, head, 0)
    local_k_ref[...] = key_grad[0:128, :]
    local_v_ref[...] = value_grad[0:128, :]
    one_ref[0:64, :] = key_grad[128:192, :].astype(BF16)
    one_ref[64:128, :] = value_grad[128:192, :].astype(BF16)
    collect(key_grad, value_grad, 0, mine_ref)
    collect(key_grad, value_grad, 1, other_ref)


def attend(*operands):
    shape = jax.ShapeDtypeStruct
    return pl.pallas_call(
        attend_kernel,
        out_shape=(
            shape((ROWS, D), BF16),
            shape((ROWS, D), BF16),
            shape((ROWS, D), F32),
            shape((ROWS, D), F32),
            shape((128, D), BF16),
            shape((320, D), F32),
            shape((320, D), BF16),
        ),
        scratch_shapes=[
            pltpu.VMEM((512, D), BF16),
            pltpu.VMEM((512, D), BF16),
            pltpu.VMEM((512, D), F32),
            pltpu.VMEM((512, D), F32),
            pltpu.VMEM((192, D), F32),
            pltpu.VMEM((192, D), F32),
        ],
        compiler_params=PARAMS,
        name="attend",
    )(*operands)


def chip_kernel(mine_ref, got_ref, near_ref, far2_ref, far3_ref, own_ref):
    start = 0
    for ref in (near_ref, far2_ref, far3_ref, own_ref):
        count = ref.shape[0]
        total = mine_ref[start : start + count, :] + got_ref[start : start + count, :].astype(F32)
        ref[...] = total.astype(ref.dtype)
        start += count


def chip_sum(mine, got):
    shape = jax.ShapeDtypeStruct
    return pl.pallas_call(
        chip_kernel,
        out_shape=(
            shape((112, D), BF16),
            shape((80, D), BF16),
            shape((80, D), BF16),
            shape((48, D), F32),
        ),
        compiler_params=PARAMS,
        name="chip_sum",
    )(mine, got)


def plane_kernel(own_ref, near_ref, far2_ref, far3_ref, send_ref):
    z = z_index()
    send_ref[z] = jnp.zeros((16, D), BF16)
    for tile in range(3):
        rows = slice(16 * tile, 16 * tile + 16)
        total = (own_ref[rows, :] + near_ref[rows, :].astype(F32)) + (
            far2_ref[rows, :].astype(F32) + far3_ref[rows, :].astype(F32)
        )
        total = total.astype(BF16)
        for other in ((1,), (2, 3), (4, 5, 6, 7))[tile]:
            send_ref[z ^ other] = total


def plane_sum(own, near, far2, far3):
    return pl.pallas_call(
        plane_kernel,
        out_shape=jax.ShapeDtypeStruct((Z, 16, D), BF16),
        compiler_params=PARAMS,
        name="plane_sum",
    )(own, near, far2, far3)


def finish_kernel(
    local_k_ref, local_v_ref, one_ref, near_ref, far2_ref, far3_ref, got_ref,
    grad_k_ref, grad_v_ref, tmp, pick,
):
    z = z_index()
    for other in range(1, Z):
        pick[16 * other : 16 * other + 16, :] = got_ref[z ^ other].astype(F32)
    for side, (local_ref, out_ref) in enumerate(
        ((local_k_ref, grad_k_ref), (local_v_ref, grad_v_ref))
    ):
        for number in range(H):
            columns = slice(number * DH, number * DH + DH)
            plane = tmp.at[side * H + number]

            def part(other, side=side, columns=columns):
                level, start = place_of(other)
                start += 16 * other + 8 * side
                return pick[start : start + (ROWS >> level), columns]

            def rows(ref, start, count, side=side, columns=columns):
                start += side * count
                return ref[start : start + count, columns].astype(F32)

            parts = {
                6: (part(4) + part(5)) + (part(6) + part(7)),
                5: part(2) + part(3),
                4: part(1),
                3: rows(far2_ref, 48, 16) + rows(far3_ref, 48, 16),
                2: rows(near_ref, 48, 32),
                1: rows(one_ref, 0, 64),
                0: local_ref[:, columns],
            }
            total = parts[6]
            for level in range(5, -1, -1):
                count = ROWS >> level
                half = total * HALF_ROOT
                plane[pl.ds(0, count // 2, stride=2), :] = half
                plane[pl.ds(1, count // 2, stride=2), :] = half
                total = plane[:count, :] + parts[level]
            out_ref[:, columns] = total.astype(BF16)


def finish(*operands):
    shape = jax.ShapeDtypeStruct
    return pl.pallas_call(
        finish_kernel,
        out_shape=(shape((ROWS, D), BF16), shape((ROWS, D), BF16)),
        scratch_shapes=[pltpu.VMEM((2 * H, ROWS, DH), F32), pltpu.VMEM((16 * Z, D), F32)],
        compiler_params=PARAMS,
        name="finish",
    )(*operands)


def per_device(queries, keys, values, cotangent):
    c1, c2, c3, send = coarsen(keys, values)
    c1 = swap(c1, 1)
    near, far = merge(z_exchange(send), c2, c3)
    own = near[:48]
    own_o = swap(own, 1)
    far2 = swap(far, 4)
    near = swap(near, 2)
    far3 = swap(far, 6)
    near_o = swap(near, 1)
    far2_o = swap(far2, 1)
    far3_o = swap(far3, 1)
    output, grad_queries, local_k, local_v, one, mine, other = attend(
        queries, keys, values, cotangent, c1,
        near, far2, far3, own, near_o, far2_o, far3_o, own_o,
    )
    got = swap(other, 1)
    one = swap(one, 1)
    near, far2, far3, own = chip_sum(mine, got)
    far2 = swap(far2, 4)
    near = swap(near, 2)
    far3 = swap(far3, 6)
    got = z_exchange(plane_sum(own, near, far2, far3))
    grad_keys, grad_values = finish(local_k, local_v, one, near, far2, far3, got)
    return output, grad_queries, grad_keys, grad_values


def solution(mesh):
    spec = P(("dp", "ctx"), None)
    return jax.shard_map(
        per_device,
        mesh=mesh,
        in_specs=(spec,) * 4,
        out_specs=(spec,) * 4,
        check_vma=False,
    )
```

```python
import jax
import jax.numpy as jnp
from jax import lax
from jax.experimental import pallas as pl
from jax.experimental.pallas import tpu as pltpu
from jax.sharding import PartitionSpec as P

H = 8
DH = 128
D = H * DH
ROWS = 128
HALF_ROOT = 0.7071067811865476
SCALE = DH ** (-0.5)
LOG2E = 1.4426950408889634
F32 = jnp.float32
BF16 = jnp.bfloat16
VMEM_LIMIT = 48 * 1024 * 1024
PARAMS = pltpu.CompilerParams(vmem_limit_bytes=VMEM_LIMIT)


def swap(block, mask):
    count = lax.axis_size("ctx")
    return lax.ppermute(block, "ctx", [(i, i ^ mask) for i in range(count)])


def coarsen_kernel(
    k_hbm, v_hbm, q_hbm, g_hbm,
    c1_ref, c2_ref, c3_ref, c4_ref, c5_ref, c6_ref, k_ref, v_ref, q_ref, g_ref,
    tmp, pack, sems,
):
    copies = [
        pltpu.make_async_copy(source, target, sems.at[number])
        for number, (source, target) in enumerate(
            ((k_hbm, k_ref), (v_hbm, v_ref), (q_hbm, q_ref), (g_hbm, g_ref))
        )
    ]
    for copy in copies:
        copy.start()
    pack[...] = jnp.zeros(pack.shape, F32)
    for side, source in enumerate((k_ref, v_ref)):
        copies[side].wait()
        for number in range(H):
            columns = slice(number * DH, number * DH + DH)
            plane = tmp.at[side * H + number]
            rows = source[:, columns].astype(F32)
            for level in range(1, 7):
                count = ROWS >> level
                plane[: 2 * count, :] = rows
                total = plane[pl.ds(0, count, stride=2), :] + plane[pl.ds(1, count, stride=2), :]
                exact = (total * HALF_ROOT).astype(BF16)
                rows = exact.astype(F32)
                if level < 4:
                    ref = (c1_ref, c2_ref, c3_ref)[level - 1]
                    ref[side * count : side * count + count, columns] = exact
                else:
                    for start in ((0,), (20,), (32, 34))[level - 4]:
                        start += 8 * side
                        pack[start : start + count, columns] = rows
    for number, ref in enumerate((c4_ref, c5_ref, c6_ref)):
        ref[...] = pack[16 * number : 16 * number + 16, :].astype(BF16)
    for copy in copies[2:]:
        copy.wait()


def coarsen(*operands):
    return pl.pallas_call(
        coarsen_kernel,
        out_shape=tuple(
            jax.ShapeDtypeStruct((count, D), BF16) for count in (128, 64, 32, 16, 16, 16) + (ROWS,) * 4
        ),
        in_specs=[pl.BlockSpec(memory_space=pltpu.HBM)] * 4,
        scratch_shapes=[
            pltpu.VMEM((2 * H, ROWS, DH), F32),
            pltpu.VMEM((48, D), F32),
            pltpu.SemaphoreType.DMA((4,)),
        ],
        compiler_params=PARAMS,
        name="coarsen",
    )(*operands)


def rows_at(first, count):
    row = lax.broadcasted_iota(jnp.int32, (16, 1), 0) % 8
    return (row >= first) & (row < first + count)


NEAR = 256
FAR = 256


def dot(a, b, a_dim, b_dim):
    return lax.dot_general(a, b, (((a_dim,), (b_dim,)), ((), ())), preferred_element_type=F32)


def by_head(body):
    def step(number, carry):
        body(pl.ds(pl.multiple_of(number * DH, DH), DH))
        return carry

    lax.fori_loop(0, H, step, 0, unroll=True)


def near_parts(c1, c2, c2_o):
    return (c1, 128, 64), (c2, 192, 32), (c2_o, 224, 32)


def near_kernel(q_ref, k_ref, v_ref, g_ref, *rest):
    parts, (key_ref, value_ref, exp_ref, dprob_ref, stats_ref) = rest[:3], rest[3:]
    key_ref[0:128, :] = k_ref[...]
    value_ref[0:128, :] = v_ref[...]
    for ref, start, count in near_parts(*parts):
        key_ref[start : start + count, :] = ref[:count, :]
        value_ref[start : start + count, :] = ref[count:, :]

    def head(columns):
        scores = dot(key_ref[:, columns], q_ref[:, columns], 1, 1)
        dprob = dot(value_ref[:, columns], g_ref[:, columns], 1, 1)
        top = jnp.max(scores, axis=0, keepdims=True)
        exponent = jnp.exp2((scores - top) * (SCALE * LOG2E))
        exp_ref[:, columns] = exponent
        dprob_ref[:, columns] = dprob
        stats_ref[0:1, columns] = top
        stats_ref[1:2, columns] = jnp.sum(exponent, axis=0, keepdims=True)
        stats_ref[2:3, columns] = jnp.sum(exponent * dprob, axis=0, keepdims=True)

    by_head(head)


def near_scores(*operands):
    shape = jax.ShapeDtypeStruct
    return pl.pallas_call(
        near_kernel,
        out_shape=(
            shape((NEAR, D), BF16),
            shape((NEAR, D), BF16),
            shape((NEAR, D), F32),
            shape((NEAR, D), F32),
            shape((8, D), F32),
        ),
        compiler_params=PARAMS,
        cost_estimate=pl.CostEstimate(
            flops=4 * NEAR * ROWS * D, bytes_accessed=8 * NEAR * D, transcendentals=NEAR * ROWS * H
        ),
        name="near_scores",
    )(*operands)


def far_kernel(q_ref, g_ref, stats_ref, *rest):
    tiles, rest = rest[:8], rest[8:]
    key_ref, value_ref, weight_ref, dscore_ref, joint_ref, mine_ref, other_ref = rest[:7]
    key_tmp, value_tmp = rest[7:]
    for number, ref in enumerate(tiles):
        for tile in range(3):
            rows = ref[16 * tile : 16 * tile + 16, :].astype(F32)
            start = 24 * number + 8 * tile
            key_tmp[start : start + 8, :] = rows[:8]
            value_tmp[start : start + 8, :] = rows[8:]
    key_ref[:192, :] = key_tmp[...].astype(BF16)
    value_ref[:192, :] = value_tmp[...].astype(BF16)
    for number, ref in enumerate((tiles[2], tiles[3], tiles[6], tiles[7])):
        start = 192 + 16 * number
        key_ref[start : start + 16, :] = ref[48:64, :]
        value_ref[start : start + 16, :] = ref[64:80, :]

    def head(columns):
        q = q_ref[:, columns]
        g = g_ref[:, columns]
        scores = dot(key_ref[:, columns], q, 1, 1)
        dprob = dot(value_ref[:, columns], g, 1, 1)
        near_top = stats_ref[0:1, columns]
        top = jnp.maximum(jnp.max(scores, axis=0, keepdims=True), near_top)
        exponent = jnp.exp2((scores - top) * (SCALE * LOG2E))
        near_factor = jnp.exp2((near_top - top) * (SCALE * LOG2E))
        total = near_factor * stats_ref[1:2, columns] + jnp.sum(exponent, axis=0, keepdims=True)
        moment = near_factor * stats_ref[2:3, columns] + jnp.sum(
            exponent * dprob, axis=0, keepdims=True
        )
        inverse = 1.0 / total
        delta = moment * inverse
        prob = exponent * inverse
        weights = prob.astype(BF16)
        dscore = (prob * (dprob - delta) * SCALE).astype(BF16)
        joint_ref[0:1, columns] = near_factor * inverse
        joint_ref[1:2, columns] = delta
        weight_ref[:, columns] = weights
        dscore_ref[:, columns] = dscore
        key_grad = dot(dscore, q, 1, 0)
        value_grad = dot(weights, g, 1, 0)
        for core, ref in enumerate((mine_ref, other_ref)):
            out = 0
            for number in range(4):
                pieces = [(96 * core + 24 * number + 8 * tile, 8) for tile in range(3)]
                if number > 1:
                    pieces.append((192 + 32 * core + 16 * (number - 2), 16))
                for start, count in pieces:
                    both = jnp.concatenate(
                        [key_grad[start : start + count], value_grad[start : start + count]], axis=0
                    )
                    ref[out : out + 2 * count, columns] = both.astype(ref.dtype)
                    out += 2 * count

    by_head(head)


def far_attend(*operands):
    shape = jax.ShapeDtypeStruct
    return pl.pallas_call(
        far_kernel,
        out_shape=(
            shape((FAR, D), BF16),
            shape((FAR, D), BF16),
            shape((FAR, D), BF16),
            shape((FAR, D), BF16),
            shape((8, D), F32),
            shape((FAR, D), F32),
            shape((FAR, D), BF16),
        ),
        scratch_shapes=[pltpu.VMEM((192, D), F32), pltpu.VMEM((192, D), F32)],
        compiler_params=PARAMS,
        cost_estimate=pl.CostEstimate(
            flops=8 * FAR * ROWS * D, bytes_accessed=8 * FAR * D, transcendentals=FAR * ROWS * H
        ),
        name="far_attend",
    )(*operands)


def rest_kernel(
    q_ref, g_ref, near_key, near_value, exp_ref, dprob_ref,
    far_key, far_value, weight_ref, dscore_ref, joint_ref,
    out_ref, grad_q_ref, local_k_ref, local_v_ref, mine_ref, other_ref,
):
    def head(columns):
        prob = exp_ref[:, columns] * joint_ref[0:1, columns]
        weights = prob.astype(BF16)
        delta = joint_ref[1:2, columns]
        dscore = (prob * (dprob_ref[:, columns] - delta) * SCALE).astype(BF16)
        output = dot(weights, near_value[:, columns], 0, 0)
        output += dot(weight_ref[:, columns], far_value[:, columns], 0, 0)
        out_ref[:, columns] = output.astype(BF16)
        grad_q = dot(dscore, near_key[:, columns], 0, 0)
        grad_q += dot(dscore_ref[:, columns], far_key[:, columns], 0, 0)
        grad_q_ref[:, columns] = grad_q.astype(BF16)
        key_grad = dot(dscore, q_ref[:, columns], 1, 0)
        value_grad = dot(weights, g_ref[:, columns], 1, 0)
        local_k_ref[:, columns] = key_grad[0:128]
        local_v_ref[:, columns] = value_grad[0:128]
        targets = ((other_ref, 0), (mine_ref, 0), (other_ref, 128))
        for (ref, out), (_, start, count) in zip(targets, near_parts(*targets)):
            ref[out : out + count, columns] = key_grad[start : start + count].astype(ref.dtype)
            out += count
            ref[out : out + count, columns] = value_grad[start : start + count].astype(ref.dtype)

    by_head(head)


def rest_attend(*operands):
    shape = jax.ShapeDtypeStruct
    return pl.pallas_call(
        rest_kernel,
        out_shape=(
            shape((ROWS, D), BF16),
            shape((ROWS, D), BF16),
            shape((ROWS, D), F32),
            shape((ROWS, D), F32),
            shape((64, D), F32),
            shape((192, D), BF16),
        ),
        compiler_params=PARAMS,
        cost_estimate=pl.CostEstimate(
            flops=4 * (2 * NEAR + FAR) * ROWS * D, bytes_accessed=16 * NEAR * D, transcendentals=0
        ),
        name="rest_attend",
    )(*operands)


def chip_kernel(mine_ref, got_ref, *pieces):
    start = 0
    skip = got_ref.shape[0] - mine_ref.shape[0]
    for ref in pieces:
        count = ref.shape[0]
        got = got_ref[skip + start : skip + start + count, :].astype(F32)
        ref[...] = (mine_ref[start : start + count, :] + got).astype(ref.dtype)
        start += count


def chip_sum(mine, got, pieces):
    return pl.pallas_call(
        chip_kernel,
        out_shape=tuple(jax.ShapeDtypeStruct((count, D), kind) for count, kind in pieces),
        compiler_params=PARAMS,
        name="chip_sum",
    )(mine, got)


def plane_kernel(own_ref, near_ref, far2_ref, far3_ref, keep_ref, send_ref):
    total = (own_ref[...] + near_ref[...].astype(F32)) + (
        far2_ref[:48, :].astype(F32) + far3_ref[:48, :].astype(F32)
    )
    keep_ref[...] = total[:16, :]
    send_ref[...] = total[16:, :].astype(BF16)


def plane_sum(own, near, far2, far3):
    return pl.pallas_call(
        plane_kernel,
        out_shape=(jax.ShapeDtypeStruct((16, D), F32), jax.ShapeDtypeStruct((32, D), BF16)),
        compiler_params=PARAMS,
        name="plane_sum",
    )(own, near, far2, far3)


def finish_kernel(
    local_k_ref, local_v_ref, c1_ref, c2_ref, far2_ref, far3_ref, z1_ref, z2_ref, z7_ref,
    grad_k_ref, grad_v_ref, tmp, pick,
):
    for number, ref in enumerate((z1_ref, z2_ref, z7_ref)):
        pick[16 * number : 16 * number + 16, :] = ref[:16, :].astype(F32)
    for side, (local_ref, out_ref) in enumerate(
        ((local_k_ref, grad_k_ref), (local_v_ref, grad_v_ref))
    ):
        for number in range(H):
            columns = slice(number * DH, number * DH + DH)
            plane = tmp.at[side * H + number]

            def part(start, count, side=side, columns=columns):
                start += 8 * side
                return pick[start : start + count, columns]

            def rows(ref, start, count, side=side, columns=columns):
                start += side * count
                return ref[start : start + count, columns].astype(F32)

            parts = {
                6: part(32, 2) + part(34, 2),
                5: part(20, 4),
                4: part(0, 8),
                3: rows(far2_ref, 48, 16) + rows(far3_ref, 48, 16),
                2: rows(c2_ref, 0, 32),
                1: rows(c1_ref, 0, 64),
                0: local_ref[:, columns],
            }
            total = parts[6]
            for level in range(5, -1, -1):
                count = ROWS >> level
                half = total * HALF_ROOT
                plane[pl.ds(0, count // 2, stride=2), :] = half
                plane[pl.ds(1, count // 2, stride=2), :] = half
                total = plane[:count, :] + parts[level]
            out_ref[:, columns] = total.astype(BF16)


def finish(*operands):
    shape = jax.ShapeDtypeStruct
    return pl.pallas_call(
        finish_kernel,
        out_shape=(shape((ROWS, D), BF16), shape((ROWS, D), BF16)),
        scratch_shapes=[pltpu.VMEM((2 * H, ROWS, DH), F32), pltpu.VMEM((48, D), F32)],
        compiler_params=PARAMS,
        name="finish",
    )(*operands)


def together(*arrays):
    return lax.optimization_barrier(arrays)


def together(*arrays):
    return lax.optimization_barrier(arrays)


def per_device(queries, keys, values, cotangent):
    pinned = [
        pltpu.with_memory_space_constraint(array, pltpu.HBM)
        for array in (keys, values, queries, cotangent)
    ]
    c1, c2, c3, c4, c5, c6, keys, values, queries, cotangent = coarsen(*pinned)
    six = swap(c6, 56)
    c1 = swap(c1, 1)
    c2 = swap(c2, 2)
    two = swap(jnp.where(rows_at(0, 2), six, c5), 16)
    keep = jnp.where(rows_at(2, 2), six, two)
    send, c2 = together(jnp.concatenate([keep, c4]), c2)
    core = swap(c2, 1)
    own = jnp.concatenate([keep, swap(send, 8)])
    own, c1, c2, core = together(own, c1, c2, core)
    far = jnp.concatenate([own, c3])
    near, far3, far2 = swap(own, 2), swap(far, 6), swap(far, 4)
    near_key, near_value, exponent, dprob, stats = near_scores(
        queries, keys, values, cotangent, c1, c2, core
    )
    near, far2, far3, stats = together(near, far2, far3, stats)
    tiles = [own, near, far2, far3]
    tiles += [swap(part, 1) for part in tiles]
    far_key, far_value, weights, dscore, joint, mine, other = far_attend(
        queries, cotangent, stats, *tiles
    )
    got = swap(other, 1)
    own, near, far2, far3 = chip_sum(mine, got, ((48, F32), (48, BF16), (80, BF16), (80, BF16)))
    joint, near, far2, far3 = together(joint, near, far2, far3)
    near, far3, far2 = swap(near, 2), swap(far3, 6), swap(far2, 4)
    output, grad_queries, local_k, local_v, mine, other = rest_attend(
        queries, cotangent, near_key, near_value, exponent, dprob,
        far_key, far_value, weights, dscore, joint,
    )
    near, far2, far3, other = together(near, far2, far3, other)
    keep, send = plane_sum(own, near, far2, far3)
    got = swap(send, 8)
    core = swap(other, 1)
    (c2,) = chip_sum(mine, core, ((64, BF16),))
    c2 = swap(c2, 2)
    keep = (keep + got[:16].astype(F32)).astype(BF16)
    two = swap(keep, 16)
    six = swap(jnp.where(rows_at(2, 2), keep, two), 56)
    grad_keys, grad_values = finish(
        local_k, local_v, core[:128], c2, far2, far3, got[16:], two, six
    )
    return output, grad_queries, grad_keys, grad_values


def solution(mesh):
    spec = P(("dp", "ctx"), None)
    return jax.shard_map(
        per_device,
        mesh=mesh,
        in_specs=(spec,) * 4,
        out_specs=(spec,) * 4,
        check_vma=False,
    )
```

```python
import jax
import jax.numpy as jnp
from jax import lax
from jax.experimental import pallas as pl
from jax.experimental.pallas import tpu as pltpu
from jax.sharding import PartitionSpec as P

H = 8
DH = 128
D = H * DH
ROWS = 128
HALF_ROOT = 0.7071067811865476
SCALE = DH ** (-0.5)
LOG2E = 1.4426950408889634
F32 = jnp.float32
BF16 = jnp.bfloat16
VMEM_LIMIT = 16 * 1024 * 1024
PARAMS = pltpu.CompilerParams(vmem_limit_bytes=VMEM_LIMIT)


def swap(block, mask):
    count = lax.axis_size("ctx")
    return lax.ppermute(block, "ctx", [(i, i ^ mask) for i in range(count)])


def coarsen_kernel(
    k_hbm, v_hbm, q_hbm, g_hbm,
    c1_ref, c2_ref, c3_ref, c4_ref, c5_ref, c6_ref, k_ref, v_ref, q_ref, g_ref,
    tmp, pack, sems,
):
    def copy(source, target, number, columns):
        return pltpu.make_async_copy(
            source.at[:, columns], target.at[:, columns], sems.at[number]
        )

    half = D // 2
    sides = ((k_hbm, k_ref), (v_hbm, v_ref))
    copies = [
        copy(source, target, 2 * part + side, pl.ds(half * part, half))
        for part in range(2)
        for side, (source, target) in enumerate(sides)
    ]
    copies.append(copy(q_hbm, q_ref, 4, pl.ds(0, D)))
    copies.append(copy(g_hbm, g_ref, 5, pl.ds(0, D)))
    for each in copies:
        each.start()
    pack[...] = jnp.zeros(pack.shape, F32)
    for part in range(4):
        copies[part].wait()
        side = part % 2
        source = sides[side][1]
        for number in range(part // 2 * (H // 2), (part // 2 + 1) * (H // 2)):
            columns = slice(number * DH, number * DH + DH)
            plane = tmp.at[side * H + number]
            rows = source[:, columns].astype(F32)
            for level in range(1, 7):
                count = ROWS >> level
                plane[: 2 * count, :] = rows
                total = plane[pl.ds(0, count, stride=2), :] + plane[pl.ds(1, count, stride=2), :]
                exact = (total * HALF_ROOT).astype(BF16)
                rows = exact.astype(F32)
                if level < 4:
                    ref = (c1_ref, c2_ref, c3_ref)[level - 1]
                    ref[side * count : side * count + count, columns] = exact
                else:
                    for start in ((0,), (20,), (32, 34))[level - 4]:
                        start += 8 * side
                        pack[start : start + count, columns] = rows
    for number, ref in enumerate((c4_ref, c5_ref, c6_ref)):
        ref[...] = pack[16 * number : 16 * number + 16, :].astype(BF16)
    for each in copies[4:]:
        each.wait()


def coarsen(*operands):
    return pl.pallas_call(
        coarsen_kernel,
        out_shape=tuple(
            jax.ShapeDtypeStruct((count, D), BF16) for count in (128, 64, 32, 16, 16, 16) + (ROWS,) * 4
        ),
        in_specs=[pl.BlockSpec(memory_space=pltpu.HBM)] * 4,
        scratch_shapes=[
            pltpu.VMEM((2 * H, ROWS, DH), F32),
            pltpu.VMEM((48, D), F32),
            pltpu.SemaphoreType.DMA((6,)),
        ],
        compiler_params=PARAMS,
        name="coarsen",
    )(*operands)


def rows_at(first, count):
    row = lax.broadcasted_iota(jnp.int32, (16, 1), 0) % 8
    return (row >= first) & (row < first + count)


NEAR = 256
FAR = 128


def dot(a, b, a_dim, b_dim):
    return lax.dot_general(a, b, (((a_dim,), (b_dim,)), ((), ())), preferred_element_type=F32)


def by_head(body):
    def step(number, carry):
        body(pl.ds(pl.multiple_of(number * DH, DH), DH))
        return carry

    lax.fori_loop(0, H, step, 0, unroll=True)


def near_parts(c1, c2, c2_o):
    return (c1, 128, 64), (c2, 192, 32), (c2_o, 224, 32)


def near_kernel(q_ref, k_ref, v_ref, g_ref, *rest):
    parts, (key_ref, value_ref, exp_ref, dprob_ref, stats_ref) = rest[:3], rest[3:]
    key_ref[0:128, :] = k_ref[...]
    value_ref[0:128, :] = v_ref[...]
    for ref, start, count in near_parts(*parts):
        key_ref[start : start + count, :] = ref[:count, :]
        value_ref[start : start + count, :] = ref[count:, :]

    def head(columns):
        scores = dot(key_ref[:, columns], q_ref[:, columns], 1, 1)
        dprob = dot(value_ref[:, columns], g_ref[:, columns], 1, 1)
        top = jnp.max(scores, axis=0, keepdims=True)
        exponent = jnp.exp2((scores - top) * (SCALE * LOG2E))
        exp_ref[:, columns] = exponent
        dprob_ref[:, columns] = dprob
        stats_ref[0:1, columns] = top
        stats_ref[1:2, columns] = jnp.sum(exponent, axis=0, keepdims=True)
        stats_ref[2:3, columns] = jnp.sum(exponent * dprob, axis=0, keepdims=True)

    by_head(head)


def near_scores(*operands):
    shape = jax.ShapeDtypeStruct
    return pl.pallas_call(
        near_kernel,
        out_shape=(
            shape((NEAR, D), BF16),
            shape((NEAR, D), BF16),
            shape((NEAR, D), F32),
            shape((NEAR, D), F32),
            shape((8, D), F32),
        ),
        compiler_params=PARAMS,
        cost_estimate=pl.CostEstimate(
            flops=4 * NEAR * ROWS * D, bytes_accessed=8 * NEAR * D, transcendentals=NEAR * ROWS * H
        ),
        name="near_scores",
    )(*operands)


def place_far(tiles, key_ref, value_ref, key_tmp, value_tmp):
    for number, (ref, base) in enumerate(tiles):
        for tile in range(3):
            rows = ref[base + 16 * tile : base + 16 * tile + 16, :].astype(F32)
            start = 24 * number + 8 * tile
            key_tmp[start : start + 8, :] = rows[:8]
            value_tmp[start : start + 8, :] = rows[8:]
    key_ref[:96, :] = key_tmp[...].astype(BF16)
    value_ref[:96, :] = value_tmp[...].astype(BF16)
    for number, (ref, base) in enumerate(tiles[2:]):
        start = 96 + 16 * number
        key_ref[start : start + 16, :] = ref[base + 48 : base + 64, :]
        value_ref[start : start + 16, :] = ref[base + 64 : base + 80, :]


def pack_far(key_grad, value_grad, ref, columns):
    out = 0
    for number in range(4):
        pieces = [(24 * number + 8 * tile, 8) for tile in range(3)]
        if number > 1:
            pieces.append((96 + 16 * (number - 2), 16))
        for start, count in pieces:
            both = jnp.concatenate(
                [key_grad[start : start + count], value_grad[start : start + count]], axis=0
            )
            ref[out : out + 2 * count, columns] = both.astype(ref.dtype)
            out += 2 * count


def power(difference):
    return jnp.exp2(difference * (SCALE * LOG2E))


def mine_kernel(
    q_ref, g_ref, stats_ref, own, near, far2, far3,
    key_ref, value_ref, exp_ref, dprob_ref, joint_ref, key_tmp, value_tmp,
):
    tiles = ((own, 0), (near, 0), (far2, 0), (far3, 0))
    place_far(tiles, key_ref, value_ref, key_tmp, value_tmp)

    def head(columns):
        scores = dot(key_ref[:, columns], q_ref[:, columns], 1, 1)
        dprob = dot(value_ref[:, columns], g_ref[:, columns], 1, 1)
        old_top = stats_ref[0:1, columns]
        top = jnp.maximum(jnp.max(scores, axis=0, keepdims=True), old_top)
        exponent = power(scores - top)
        factor = power(old_top - top)
        exp_ref[:, columns] = exponent
        dprob_ref[:, columns] = dprob
        joint_ref[0:1, columns] = top
        joint_ref[1:2, columns] = factor * stats_ref[1:2, columns] + jnp.sum(
            exponent, axis=0, keepdims=True
        )
        joint_ref[2:3, columns] = factor * stats_ref[2:3, columns] + jnp.sum(
            exponent * dprob, axis=0, keepdims=True
        )
        joint_ref[3:4, columns] = factor

    by_head(head)


FAR_COST = pl.CostEstimate(
    flops=4 * FAR * ROWS * D, bytes_accessed=16 * FAR * D, transcendentals=FAR * ROWS * H
)
FAR_TMP = [pltpu.VMEM((96, D), F32), pltpu.VMEM((96, D), F32)]


def mine_scores(*operands):
    shape = jax.ShapeDtypeStruct
    return pl.pallas_call(
        mine_kernel,
        out_shape=(
            shape((FAR, D), BF16),
            shape((FAR, D), BF16),
            shape((FAR, D), F32),
            shape((FAR, D), F32),
            shape((8, D), F32),
        ),
        scratch_shapes=FAR_TMP,
        compiler_params=PARAMS,
        cost_estimate=FAR_COST,
        name="mine_scores",
    )(*operands)


def other_kernel(
    q_ref, g_ref, joint_ref, early, late,
    key_ref, value_ref, weight_ref, dscore_ref, final_ref, grad_ref,
    key_tmp, value_tmp, score_tmp, dprob_tmp,
):
    tiles = ((early, 0), (early, 48), (late, 0), (late, 80))
    place_far(tiles, key_ref, value_ref, key_tmp, value_tmp)

    def scores_of(columns):
        score_tmp[:, columns] = dot(key_ref[:, columns], q_ref[:, columns], 1, 1)
        dprob_tmp[:, columns] = dot(value_ref[:, columns], g_ref[:, columns], 1, 1)

    by_head(scores_of)
    old_top = joint_ref[0:1, :]
    top = jnp.maximum(jnp.max(score_tmp[...], axis=0, keepdims=True), old_top)
    factor = power(old_top - top)
    exponent = power(score_tmp[...] - top)
    dprob = dprob_tmp[...]
    total = factor * joint_ref[1:2, :] + jnp.sum(exponent, axis=0, keepdims=True)
    moment = factor * joint_ref[2:3, :] + jnp.sum(exponent * dprob, axis=0, keepdims=True)
    inverse = 1.0 / total
    delta = moment * inverse
    prob = exponent * inverse
    weight_ref[...] = prob.astype(BF16)
    dscore_ref[...] = (prob * (dprob - delta) * SCALE).astype(BF16)
    mine_factor = factor * inverse
    final_ref[0:1, :] = mine_factor * joint_ref[3:4, :]
    final_ref[1:2, :] = mine_factor
    final_ref[2:3, :] = delta

    def grads_of(columns):
        key_grad = dot(dscore_ref[:, columns], q_ref[:, columns], 1, 0)
        value_grad = dot(weight_ref[:, columns], g_ref[:, columns], 1, 0)
        pack_far(key_grad, value_grad, grad_ref, columns)

    by_head(grads_of)


def other_attend(*operands):
    shape = jax.ShapeDtypeStruct
    return pl.pallas_call(
        other_kernel,
        out_shape=(
            shape((FAR, D), BF16),
            shape((FAR, D), BF16),
            shape((FAR, D), BF16),
            shape((FAR, D), BF16),
            shape((8, D), F32),
            shape((2 * FAR, D), BF16),
        ),
        scratch_shapes=FAR_TMP + [pltpu.VMEM((FAR, D), F32), pltpu.VMEM((FAR, D), F32)],
        compiler_params=PARAMS,
        cost_estimate=FAR_COST,
        name="other_attend",
    )(*operands)


def soften(exp_ref, dprob_ref, final_ref, row, columns):
    prob = exp_ref[:, columns] * final_ref[row : row + 1, columns]
    dscore = prob * (dprob_ref[:, columns] - final_ref[2:3, columns]) * SCALE
    return prob.astype(BF16), dscore.astype(BF16)


def mine_grad_kernel(q_ref, g_ref, exp_ref, dprob_ref, final_ref, weight_ref, dscore_ref, grad_ref):
    def head(columns):
        weights, dscore = soften(exp_ref, dprob_ref, final_ref, 1, columns)
        weight_ref[:, columns] = weights
        dscore_ref[:, columns] = dscore
        key_grad = dot(dscore, q_ref[:, columns], 1, 0)
        pack_far(key_grad, dot(weights, g_ref[:, columns], 1, 0), grad_ref, columns)

    by_head(head)


def mine_grads(*operands):
    shape = jax.ShapeDtypeStruct
    return pl.pallas_call(
        mine_grad_kernel,
        out_shape=(shape((FAR, D), BF16), shape((FAR, D), BF16), shape((2 * FAR, D), F32)),
        compiler_params=PARAMS,
        cost_estimate=FAR_COST,
        name="mine_grads",
    )(*operands)


def near_grad_kernel(
    q_ref, g_ref, exp_ref, dprob_ref, final_ref,
    weight_ref, dscore_ref, local_k_ref, local_v_ref, mine_ref, other_ref,
):
    def head(columns):
        weights, dscore = soften(exp_ref, dprob_ref, final_ref, 0, columns)
        weight_ref[:, columns] = weights
        dscore_ref[:, columns] = dscore
        key_grad = dot(dscore, q_ref[:, columns], 1, 0)
        value_grad = dot(weights, g_ref[:, columns], 1, 0)
        local_k_ref[:, columns] = key_grad[0:128]
        local_v_ref[:, columns] = value_grad[0:128]
        targets = ((other_ref, 0), (mine_ref, 0), (other_ref, 128))
        for (ref, out), (_, start, count) in zip(targets, near_parts(*targets)):
            ref[out : out + count, columns] = key_grad[start : start + count].astype(ref.dtype)
            out += count
            ref[out : out + count, columns] = value_grad[start : start + count].astype(ref.dtype)

    by_head(head)


def near_grads(*operands):
    shape = jax.ShapeDtypeStruct
    return pl.pallas_call(
        near_grad_kernel,
        out_shape=(
            shape((NEAR, D), BF16),
            shape((NEAR, D), BF16),
            shape((ROWS, D), F32),
            shape((ROWS, D), F32),
            shape((64, D), F32),
            shape((192, D), BF16),
        ),
        compiler_params=PARAMS,
        cost_estimate=pl.CostEstimate(
            flops=4 * NEAR * ROWS * D, bytes_accessed=16 * NEAR * D, transcendentals=0
        ),
        name="near_grads",
    )(*operands)


def output_kernel(*refs):
    sets, (out_ref, grad_q_ref) = (refs[0:4], refs[4:8], refs[8:12]), refs[12:]

    def head(columns):
        output = grad_q = 0.0
        for key, value, weights, dscore in sets:
            output += dot(weights[:, columns], value[:, columns], 0, 0)
            grad_q += dot(dscore[:, columns], key[:, columns], 0, 0)
        out_ref[:, columns] = output.astype(BF16)
        grad_q_ref[:, columns] = grad_q.astype(BF16)

    by_head(head)


def outputs(*operands):
    shape = jax.ShapeDtypeStruct
    return pl.pallas_call(
        output_kernel,
        out_shape=(shape((ROWS, D), BF16), shape((ROWS, D), BF16)),
        compiler_params=PARAMS,
        cost_estimate=pl.CostEstimate(
            flops=8 * NEAR * ROWS * D, bytes_accessed=16 * NEAR * D, transcendentals=0
        ),
        name="outputs",
    )(*operands)


def chip_kernel(mine_ref, got_ref, *pieces):
    start = 0
    skip = got_ref.shape[0] - mine_ref.shape[0]
    for ref in pieces:
        count = ref.shape[0]
        got = got_ref[skip + start : skip + start + count, :].astype(F32)
        ref[...] = (mine_ref[start : start + count, :] + got).astype(ref.dtype)
        start += count


def chip_sum(mine, got, pieces):
    return pl.pallas_call(
        chip_kernel,
        out_shape=tuple(jax.ShapeDtypeStruct((count, D), kind) for count, kind in pieces),
        compiler_params=PARAMS,
        name="chip_sum",
    )(mine, got)


def plane_kernel(own_ref, near_ref, far2_ref, far3_ref, keep_ref, send_ref):
    total = (own_ref[...] + near_ref[...].astype(F32)) + (
        far2_ref[...].astype(F32) + far3_ref[:48, :].astype(F32)
    )
    keep_ref[...] = total[:16, :]
    send_ref[...] = total[16:, :].astype(BF16)


def plane_sum(own, near, far2, far3):
    return pl.pallas_call(
        plane_kernel,
        out_shape=(jax.ShapeDtypeStruct((16, D), F32), jax.ShapeDtypeStruct((32, D), BF16)),
        compiler_params=PARAMS,
        name="plane_sum",
    )(own, near, far2, far3)


def finish_kernel(
    local_k_ref, local_v_ref, c1_ref, c2_ref, c3_ref, far3_ref, z1_ref, z2_ref, z7_ref,
    grad_k_ref, grad_v_ref, tmp, pick,
):
    for number, ref in enumerate((z1_ref, z2_ref, z7_ref)):
        pick[16 * number : 16 * number + 16, :] = ref[:16, :].astype(F32)
    for side, (local_ref, out_ref) in enumerate(
        ((local_k_ref, grad_k_ref), (local_v_ref, grad_v_ref))
    ):
        for number in range(H):
            columns = slice(number * DH, number * DH + DH)
            plane = tmp.at[side * H + number]

            def part(start, count, side=side, columns=columns):
                start += 8 * side
                return pick[start : start + count, columns]

            def rows(ref, start, count, side=side, columns=columns):
                start += side * count
                return ref[start : start + count, columns].astype(F32)

            parts = {
                6: part(32, 2) + part(34, 2),
                5: part(20, 4),
                4: part(0, 8),
                3: rows(c3_ref, 0, 16) + rows(far3_ref, 48, 16),
                2: rows(c2_ref, 0, 32),
                1: rows(c1_ref, 0, 64),
                0: local_ref[:, columns],
            }
            total = parts[6]
            for level in range(5, -1, -1):
                count = ROWS >> level
                half = total * HALF_ROOT
                plane[pl.ds(0, count // 2, stride=2), :] = half
                plane[pl.ds(1, count // 2, stride=2), :] = half
                total = plane[:count, :] + parts[level]
            out_ref[:, columns] = total.astype(BF16)


def finish(*operands):
    shape = jax.ShapeDtypeStruct
    return pl.pallas_call(
        finish_kernel,
        out_shape=(shape((ROWS, D), BF16), shape((ROWS, D), BF16)),
        scratch_shapes=[pltpu.VMEM((2 * H, ROWS, DH), F32), pltpu.VMEM((48, D), F32)],
        compiler_params=PARAMS,
        name="finish",
    )(*operands)


def together(*arrays):
    return lax.optimization_barrier(arrays)


def together(*arrays):
    return lax.optimization_barrier(arrays)


def per_device(queries, keys, values, cotangent):
    pinned = [
        pltpu.with_memory_space_constraint(array, pltpu.HBM)
        for array in (keys, values, queries, cotangent)
    ]
    c1, c2, c3, c4, c5, c6, keys, values, queries, cotangent = coarsen(*pinned)
    six = swap(c6, 56)
    c1 = swap(c1, 1)
    c2 = swap(c2, 2)
    two = swap(jnp.where(rows_at(0, 2), six, c5), 16)
    keep = jnp.where(rows_at(2, 2), six, two)
    send, c2 = together(jnp.concatenate([keep, c4]), c2)
    core = swap(c2, 1)
    own = jnp.concatenate([keep, swap(send, 8)])
    own, c1, c2, core = together(own, c1, c2, core)
    far = jnp.concatenate([own, c3])
    near, far3, far2 = swap(own, 2), swap(far, 6), swap(far, 4)
    near_key, near_value, exponent, dprob, stats = near_scores(
        queries, keys, values, cotangent, c1, c2, core
    )
    early = swap(jnp.concatenate([own, near]), 1)
    far3, stats = together(far3, stats)
    late = swap(jnp.concatenate([far2, far3]), 1)
    mine_key, mine_value, mine_exponent, mine_dprob, joint = mine_scores(
        queries, cotangent, stats, own, near, far2, far3
    )
    joint, *core = together(joint, early, late)
    other_key, other_value, other_weights, other_dscore, final, other = other_attend(
        queries, cotangent, joint, *core
    )
    got = swap(other, 1)
    mine_weights, mine_dscore, mine = mine_grads(
        queries, cotangent, mine_exponent, mine_dprob, final
    )
    got, mine = together(got, mine)
    own, near, far2, c3a, far3 = chip_sum(
        mine, got, ((48, F32), (48, BF16), (48, BF16), (32, BF16), (80, BF16))
    )
    final, near, far2, far3 = together(final, near, far2, far3)
    near, far3, far2 = swap(near, 2), swap(far3, 6), swap(far2, 4)
    near_weights, near_dscore, local_k, local_v, mine, other = near_grads(
        queries, cotangent, exponent, dprob, final
    )
    near, far3, far2, other = together(near, far3, far2, other)
    keep, send = plane_sum(own, near, far2, far3)
    send, near_weights, c3a = together(send, near_weights, c3a)
    got = swap(send, 8)
    output, grad_queries = outputs(
        near_key, near_value, near_weights, near_dscore,
        mine_key, mine_value, mine_weights, mine_dscore,
        other_key, other_value, other_weights, other_dscore,
    )
    got, output = together(got, output)
    core = swap(other, 1)
    (c2,) = chip_sum(mine, core, ((64, BF16),))
    c2 = swap(c2, 2)
    c3a = swap(c3a, 4)
    keep = (keep + got[:16].astype(F32)).astype(BF16)
    two = swap(keep, 16)
    six = swap(jnp.where(rows_at(2, 2), keep, two), 56)
    grad_keys, grad_values = finish(
        local_k, local_v, core[:128], c2, c3a, far3, got[16:], two, six
    )
    return output, grad_queries, grad_keys, grad_values


def solution(mesh):
    spec = P(("dp", "ctx"), None)
    return jax.shard_map(
        per_device,
        mesh=mesh,
        in_specs=(spec,) * 4,
        out_specs=(spec,) * 4,
        check_vma=False,
    )
```

```python
import jax
import jax.numpy as jnp
from jax import lax
from jax.experimental import pallas as pl
from jax.experimental.pallas import tpu as pltpu
from jax.sharding import PartitionSpec as P

H = 8
DH = 128
D = H * DH
ROWS = 128
HALF_ROOT = 0.7071067811865476
SCALE = DH ** (-0.5)
LOG2E = 1.4426950408889634
F32 = jnp.float32
BF16 = jnp.bfloat16
VMEM_LIMIT = 16 * 1024 * 1024
PARAMS = pltpu.CompilerParams(vmem_limit_bytes=VMEM_LIMIT)


def swap(block, mask):
    count = lax.axis_size("ctx")
    return lax.ppermute(block, "ctx", [(i, i ^ mask) for i in range(count)])


def coarsen_kernel(
    k_hbm, v_hbm, q_hbm, g_hbm,
    c1_ref, c2_ref, c3_ref, c4_ref, c5_ref, c6_ref, k_ref, v_ref, q_ref, g_ref,
    tmp, pack, sems,
):
    def copy(source, target, number, columns):
        return pltpu.make_async_copy(
            source.at[:, columns], target.at[:, columns], sems.at[number]
        )

    half = D // 2
    sides = ((k_hbm, k_ref), (v_hbm, v_ref))
    copies = [
        copy(source, target, 2 * part + side, pl.ds(half * part, half))
        for part in range(2)
        for side, (source, target) in enumerate(sides)
    ]
    copies.append(copy(q_hbm, q_ref, 4, pl.ds(0, D)))
    copies.append(copy(g_hbm, g_ref, 5, pl.ds(0, D)))
    for each in copies:
        each.start()
    pack[...] = jnp.zeros(pack.shape, F32)
    for part in range(4):
        copies[part].wait()
        side = part % 2
        source = sides[side][1]
        for number in range(part // 2 * (H // 2), (part // 2 + 1) * (H // 2)):
            columns = slice(number * DH, number * DH + DH)
            plane = tmp.at[side * H + number]
            rows = source[:, columns].astype(F32)
            for level in range(1, 7):
                count = ROWS >> level
                plane[: 2 * count, :] = rows
                total = plane[pl.ds(0, count, stride=2), :] + plane[pl.ds(1, count, stride=2), :]
                exact = (total * HALF_ROOT).astype(BF16)
                rows = exact.astype(F32)
                if level < 4:
                    ref = (c1_ref, c2_ref, c3_ref)[level - 1]
                    ref[side * count : side * count + count, columns] = exact
                else:
                    for start in ((0,), (20,), (32, 34))[level - 4]:
                        start += 8 * side
                        pack[start : start + count, columns] = rows
    for number, ref in enumerate((c4_ref, c5_ref, c6_ref)):
        ref[...] = pack[16 * number : 16 * number + 16, :].astype(BF16)
    for each in copies[4:]:
        each.wait()


def coarsen(*operands):
    return pl.pallas_call(
        coarsen_kernel,
        out_shape=tuple(
            jax.ShapeDtypeStruct((count, D), BF16) for count in (128, 64, 32, 16, 16, 16) + (ROWS,) * 4
        ),
        in_specs=[pl.BlockSpec(memory_space=pltpu.HBM)] * 4,
        scratch_shapes=[
            pltpu.VMEM((2 * H, ROWS, DH), F32),
            pltpu.VMEM((48, D), F32),
            pltpu.SemaphoreType.DMA((6,)),
        ],
        compiler_params=PARAMS,
        name="coarsen",
    )(*operands)


def rows_at(first, count):
    row = lax.broadcasted_iota(jnp.int32, (16, 1), 0) % 8
    return (row >= first) & (row < first + count)


NEAR = 256
FAR = 128


def dot(a, b, a_dim, b_dim):
    return lax.dot_general(a, b, (((a_dim,), (b_dim,)), ((), ())), preferred_element_type=F32)


def by_head(body):
    def step(number, carry):
        body(pl.ds(pl.multiple_of(number * DH, DH), DH))
        return carry

    lax.fori_loop(0, H, step, 0, unroll=True)


def near_parts(c1, c2, c2_o):
    return (c1, 128, 64), (c2, 192, 32), (c2_o, 224, 32)


def near_kernel(q_ref, k_ref, v_ref, g_ref, *rest):
    parts, (key_ref, value_ref, exp_ref, dprob_ref, stats_ref) = rest[:3], rest[3:]
    key_ref[0:128, :] = k_ref[...]
    value_ref[0:128, :] = v_ref[...]
    for ref, start, count in near_parts(*parts):
        key_ref[start : start + count, :] = ref[:count, :]
        value_ref[start : start + count, :] = ref[count:, :]

    def head(columns):
        scores = dot(key_ref[:, columns], q_ref[:, columns], 1, 1)
        dprob = dot(value_ref[:, columns], g_ref[:, columns], 1, 1)
        top = jnp.max(scores, axis=0, keepdims=True)
        exponent = jnp.exp2((scores - top) * (SCALE * LOG2E))
        exp_ref[:, columns] = exponent
        dprob_ref[:, columns] = dprob
        stats_ref[0:1, columns] = top
        stats_ref[1:2, columns] = jnp.sum(exponent, axis=0, keepdims=True)
        stats_ref[2:3, columns] = jnp.sum(exponent * dprob, axis=0, keepdims=True)

    by_head(head)


def near_scores(*operands):
    shape = jax.ShapeDtypeStruct
    return pl.pallas_call(
        near_kernel,
        out_shape=(
            shape((NEAR, D), BF16),
            shape((NEAR, D), BF16),
            shape((NEAR, D), F32),
            shape((NEAR, D), F32),
            shape((8, D), F32),
        ),
        compiler_params=PARAMS,
        cost_estimate=pl.CostEstimate(
            flops=4 * NEAR * ROWS * D, bytes_accessed=8 * NEAR * D, transcendentals=NEAR * ROWS * H
        ),
        name="near_scores",
    )(*operands)


def place_far(tiles, key_ref, value_ref, key_tmp, value_tmp):
    for number, (ref, base) in enumerate(tiles):
        for tile in range(3):
            rows = ref[base + 16 * tile : base + 16 * tile + 16, :].astype(F32)
            start = 24 * number + 8 * tile
            key_tmp[start : start + 8, :] = rows[:8]
            value_tmp[start : start + 8, :] = rows[8:]
    key_ref[:96, :] = key_tmp[...].astype(BF16)
    value_ref[:96, :] = value_tmp[...].astype(BF16)
    for number, (ref, base) in enumerate(tiles[2:]):
        start = 96 + 16 * number
        key_ref[start : start + 16, :] = ref[base + 48 : base + 64, :]
        value_ref[start : start + 16, :] = ref[base + 64 : base + 80, :]


def pack_far(key_grad, value_grad, ref, columns):
    out = 0
    for number in range(4):
        pieces = [(24 * number + 8 * tile, 8) for tile in range(3)]
        if number > 1:
            pieces.append((96 + 16 * (number - 2), 16))
        for start, count in pieces:
            both = jnp.concatenate(
                [key_grad[start : start + count], value_grad[start : start + count]], axis=0
            )
            ref[out : out + 2 * count, columns] = both.astype(ref.dtype)
            out += 2 * count


def power(difference):
    return jnp.exp2(difference * (SCALE * LOG2E))


def mine_kernel(
    q_ref, g_ref, stats_ref, own, near, far2, far3,
    key_ref, value_ref, exp_ref, dprob_ref, joint_ref, key_tmp, value_tmp,
):
    tiles = ((own, 0), (near, 0), (far2, 0), (far3, 0))
    place_far(tiles, key_ref, value_ref, key_tmp, value_tmp)

    def head(columns):
        scores = dot(key_ref[:, columns], q_ref[:, columns], 1, 1)
        dprob = dot(value_ref[:, columns], g_ref[:, columns], 1, 1)
        old_top = stats_ref[0:1, columns]
        top = jnp.maximum(jnp.max(scores, axis=0, keepdims=True), old_top)
        exponent = power(scores - top)
        factor = power(old_top - top)
        exp_ref[:, columns] = exponent
        dprob_ref[:, columns] = dprob
        joint_ref[0:1, columns] = top
        joint_ref[1:2, columns] = factor * stats_ref[1:2, columns] + jnp.sum(
            exponent, axis=0, keepdims=True
        )
        joint_ref[2:3, columns] = factor * stats_ref[2:3, columns] + jnp.sum(
            exponent * dprob, axis=0, keepdims=True
        )
        joint_ref[3:4, columns] = factor

    by_head(head)


FAR_COST = pl.CostEstimate(
    flops=4 * FAR * ROWS * D, bytes_accessed=16 * FAR * D, transcendentals=FAR * ROWS * H
)
FAR_TMP = [pltpu.VMEM((96, D), F32), pltpu.VMEM((96, D), F32)]


def mine_scores(*operands):
    shape = jax.ShapeDtypeStruct
    return pl.pallas_call(
        mine_kernel,
        out_shape=(
            shape((FAR, D), BF16),
            shape((FAR, D), BF16),
            shape((FAR, D), F32),
            shape((FAR, D), F32),
            shape((8, D), F32),
        ),
        scratch_shapes=FAR_TMP,
        compiler_params=PARAMS,
        cost_estimate=FAR_COST,
        name="mine_scores",
    )(*operands)


def other_kernel(
    q_ref, g_ref, joint_ref, early, late,
    key_ref, value_ref, weight_ref, dscore_ref, final_ref, grad_ref,
    key_tmp, value_tmp, score_tmp, dprob_tmp,
):
    tiles = ((early, 0), (early, 48), (late, 0), (late, 80))
    place_far(tiles, key_ref, value_ref, key_tmp, value_tmp)

    def scores_of(columns):
        score_tmp[:, columns] = dot(key_ref[:, columns], q_ref[:, columns], 1, 1)
        dprob_tmp[:, columns] = dot(value_ref[:, columns], g_ref[:, columns], 1, 1)

    by_head(scores_of)
    old_top = joint_ref[0:1, :]
    top = jnp.maximum(jnp.max(score_tmp[...], axis=0, keepdims=True), old_top)
    factor = power(old_top - top)
    exponent = power(score_tmp[...] - top)
    dprob = dprob_tmp[...]
    total = factor * joint_ref[1:2, :] + jnp.sum(exponent, axis=0, keepdims=True)
    moment = factor * joint_ref[2:3, :] + jnp.sum(exponent * dprob, axis=0, keepdims=True)
    inverse = 1.0 / total
    delta = moment * inverse
    prob = exponent * inverse
    weight_ref[...] = prob.astype(BF16)
    dscore_ref[...] = (prob * (dprob - delta) * SCALE).astype(BF16)
    mine_factor = factor * inverse
    final_ref[0:1, :] = mine_factor * joint_ref[3:4, :]
    final_ref[1:2, :] = mine_factor
    final_ref[2:3, :] = delta

    def grads_of(columns):
        key_grad = dot(dscore_ref[:, columns], q_ref[:, columns], 1, 0)
        value_grad = dot(weight_ref[:, columns], g_ref[:, columns], 1, 0)
        pack_far(key_grad, value_grad, grad_ref, columns)

    by_head(grads_of)


def other_attend(*operands):
    shape = jax.ShapeDtypeStruct
    return pl.pallas_call(
        other_kernel,
        out_shape=(
            shape((FAR, D), BF16),
            shape((FAR, D), BF16),
            shape((FAR, D), BF16),
            shape((FAR, D), BF16),
            shape((8, D), F32),
            shape((2 * FAR, D), BF16),
        ),
        scratch_shapes=FAR_TMP + [pltpu.VMEM((FAR, D), F32), pltpu.VMEM((FAR, D), F32)],
        compiler_params=PARAMS,
        cost_estimate=FAR_COST,
        name="other_attend",
    )(*operands)


def soften(exp_ref, dprob_ref, final_ref, row, columns):
    prob = exp_ref[:, columns] * final_ref[row : row + 1, columns]
    dscore = prob * (dprob_ref[:, columns] - final_ref[2:3, columns]) * SCALE
    return prob.astype(BF16), dscore.astype(BF16)


def mine_grad_kernel(q_ref, g_ref, exp_ref, dprob_ref, final_ref, weight_ref, dscore_ref, grad_ref):
    def head(columns):
        weights, dscore = soften(exp_ref, dprob_ref, final_ref, 1, columns)
        weight_ref[:, columns] = weights
        dscore_ref[:, columns] = dscore
        key_grad = dot(dscore, q_ref[:, columns], 1, 0)
        pack_far(key_grad, dot(weights, g_ref[:, columns], 1, 0), grad_ref, columns)

    by_head(head)


def mine_grads(*operands):
    shape = jax.ShapeDtypeStruct
    return pl.pallas_call(
        mine_grad_kernel,
        out_shape=(shape((FAR, D), BF16), shape((FAR, D), BF16), shape((2 * FAR, D), F32)),
        compiler_params=PARAMS,
        cost_estimate=FAR_COST,
        name="mine_grads",
    )(*operands)


def near_grad_kernel(
    q_ref, g_ref, exp_ref, dprob_ref, final_ref,
    weight_ref, dscore_ref, local_k_ref, local_v_ref, mine_ref, other_ref,
):
    def head(columns):
        weights, dscore = soften(exp_ref, dprob_ref, final_ref, 0, columns)
        weight_ref[:, columns] = weights
        dscore_ref[:, columns] = dscore
        key_grad = dot(dscore, q_ref[:, columns], 1, 0)
        value_grad = dot(weights, g_ref[:, columns], 1, 0)
        local_k_ref[:, columns] = key_grad[0:128]
        local_v_ref[:, columns] = value_grad[0:128]
        targets = ((other_ref, 0), (mine_ref, 0), (other_ref, 128))
        for (ref, out), (_, start, count) in zip(targets, near_parts(*targets)):
            ref[out : out + count, columns] = key_grad[start : start + count].astype(ref.dtype)
            out += count
            ref[out : out + count, columns] = value_grad[start : start + count].astype(ref.dtype)

    by_head(head)


def near_grads(*operands):
    shape = jax.ShapeDtypeStruct
    return pl.pallas_call(
        near_grad_kernel,
        out_shape=(
            shape((NEAR, D), BF16),
            shape((NEAR, D), BF16),
            shape((ROWS, D), F32),
            shape((ROWS, D), F32),
            shape((64, D), F32),
            shape((192, D), BF16),
        ),
        compiler_params=PARAMS,
        cost_estimate=pl.CostEstimate(
            flops=4 * NEAR * ROWS * D, bytes_accessed=16 * NEAR * D, transcendentals=0
        ),
        name="near_grads",
    )(*operands)


def output_kernel(*refs):
    sets, (out_ref, grad_q_ref) = (refs[0:4], refs[4:8], refs[8:12]), refs[12:]

    def head(columns):
        output = grad_q = 0.0
        for key, value, weights, dscore in sets:
            output += dot(weights[:, columns], value[:, columns], 0, 0)
            grad_q += dot(dscore[:, columns], key[:, columns], 0, 0)
        out_ref[:, columns] = output.astype(BF16)
        grad_q_ref[:, columns] = grad_q.astype(BF16)

    by_head(head)


def outputs(*operands):
    shape = jax.ShapeDtypeStruct
    return pl.pallas_call(
        output_kernel,
        out_shape=(shape((ROWS, D), BF16), shape((ROWS, D), BF16)),
        compiler_params=PARAMS,
        cost_estimate=pl.CostEstimate(
            flops=8 * NEAR * ROWS * D, bytes_accessed=16 * NEAR * D, transcendentals=0
        ),
        name="outputs",
    )(*operands)


def chip_kernel(mine_ref, got_ref, *pieces):
    start = 0
    skip = got_ref.shape[0] - mine_ref.shape[0]
    for ref in pieces:
        count = ref.shape[0]
        got = got_ref[skip + start : skip + start + count, :].astype(F32)
        ref[...] = (mine_ref[start : start + count, :] + got).astype(ref.dtype)
        start += count


def chip_sum(mine, got, pieces):
    return pl.pallas_call(
        chip_kernel,
        out_shape=tuple(jax.ShapeDtypeStruct((count, D), kind) for count, kind in pieces),
        compiler_params=PARAMS,
        name="chip_sum",
    )(mine, got)


def plane_kernel(own_ref, near_ref, far2_ref, far3_ref, keep_ref, send_ref):
    total = (own_ref[...] + near_ref[...].astype(F32)) + (
        far2_ref[...].astype(F32) + far3_ref[:48, :].astype(F32)
    )
    keep_ref[...] = total[:16, :]
    send_ref[...] = total[16:, :].astype(BF16)


def plane_sum(own, near, far2, far3):
    return pl.pallas_call(
        plane_kernel,
        out_shape=(jax.ShapeDtypeStruct((16, D), F32), jax.ShapeDtypeStruct((32, D), BF16)),
        compiler_params=PARAMS,
        name="plane_sum",
    )(own, near, far2, far3)


def gather_kernel(
    local_k_ref, local_v_ref, c1_ref, c2_ref, c3_ref, far3_ref, z1_ref, z2_ref,
    grad_k_ref, grad_v_ref, tmp, pick,
):
    for number, ref in enumerate((z1_ref, z2_ref)):
        pick[16 * number : 16 * number + 16, :] = ref[...].astype(F32)
    for side, (local_ref, out_ref) in enumerate(
        ((local_k_ref, grad_k_ref), (local_v_ref, grad_v_ref))
    ):
        for number in range(H):
            columns = slice(number * DH, number * DH + DH)
            plane = tmp.at[side * H + number]

            def rows(ref, start, count, side=side, columns=columns):
                start += side * count
                return ref[start : start + count, columns].astype(F32)

            parts = {
                5: pick[20 + 8 * side : 24 + 8 * side, columns],
                4: rows(pick, 0, 8),
                3: rows(c3_ref, 0, 16) + rows(far3_ref, 48, 16),
                2: rows(c2_ref, 0, 32),
                1: rows(c1_ref, 0, 64),
                0: local_ref[:, columns],
            }
            total = parts[5]
            for level in range(4, -1, -1):
                count = ROWS >> level
                half = total * HALF_ROOT
                plane[pl.ds(0, count // 2, stride=2), :] = half
                plane[pl.ds(1, count // 2, stride=2), :] = half
                total = plane[:count, :] + parts[level]
            out_ref[:, columns] = total


def gather(*operands):
    shape = jax.ShapeDtypeStruct
    return pl.pallas_call(
        gather_kernel,
        out_shape=(shape((ROWS, D), F32), shape((ROWS, D), F32)),
        scratch_shapes=[pltpu.VMEM((2 * H, ROWS, DH), F32), pltpu.VMEM((32, D), F32)],
        compiler_params=PARAMS,
        cost_estimate=FAR_COST,
        name="gather",
    )(*operands)


def finish_kernel(part_k_ref, part_v_ref, z7_ref, grad_k_ref, grad_v_ref):
    top = z7_ref[...].astype(F32)
    for side, (part_ref, out_ref) in enumerate(
        ((part_k_ref, grad_k_ref), (part_v_ref, grad_v_ref))
    ):
        for row in range(2):
            first = 8 * side + row
            both = top[first : first + 1] + top[first + 2 : first + 3]
            rows = slice(64 * row, 64 * row + 64)
            out_ref[rows, :] = (part_ref[rows, :] + both * 0.125).astype(BF16)


def finish(*operands):
    shape = jax.ShapeDtypeStruct
    return pl.pallas_call(
        finish_kernel,
        out_shape=(shape((ROWS, D), BF16), shape((ROWS, D), BF16)),
        compiler_params=PARAMS,
        name="finish",
    )(*operands)


def together(*arrays):
    return lax.optimization_barrier(arrays)


def together(*arrays):
    return lax.optimization_barrier(arrays)


def per_device(queries, keys, values, cotangent):
    pinned = [
        pltpu.with_memory_space_constraint(array, pltpu.HBM)
        for array in (keys, values, queries, cotangent)
    ]
    c1, c2, c3, c4, c5, c6, keys, values, queries, cotangent = coarsen(*pinned)
    six = swap(c6, 56)
    c1 = swap(c1, 1)
    c2 = swap(c2, 2)
    two = swap(jnp.where(rows_at(0, 2), six, c5), 16)
    keep = jnp.where(rows_at(2, 2), six, two)
    send, c2 = together(jnp.concatenate([keep, c4]), c2)
    core = swap(c2, 1)
    own = jnp.concatenate([keep, swap(send, 8)])
    own, c1, c2, core = together(own, c1, c2, core)
    far = jnp.concatenate([own, c3])
    near, far3, far2 = swap(own, 2), swap(far, 6), swap(far, 4)
    near_key, near_value, exponent, dprob, stats = near_scores(
        queries, keys, values, cotangent, c1, c2, core
    )
    early = swap(jnp.concatenate([own, near]), 1)
    far3, stats = together(far3, stats)
    late = swap(jnp.concatenate([far2, far3]), 1)
    mine_key, mine_value, mine_exponent, mine_dprob, joint = mine_scores(
        queries, cotangent, stats, own, near, far2, far3
    )
    joint, *core = together(joint, early, late)
    other_key, other_value, other_weights, other_dscore, final, other = other_attend(
        queries, cotangent, joint, *core
    )
    got = swap(other, 1)
    mine_weights, mine_dscore, mine = mine_grads(
        queries, cotangent, mine_exponent, mine_dprob, final
    )
    got, mine = together(got, mine)
    own, near, far2, c3a, far3 = chip_sum(
        mine, got, ((48, F32), (48, BF16), (48, BF16), (32, BF16), (80, BF16))
    )
    final, near, far2, far3 = together(final, near, far2, far3)
    near, far3, far2 = swap(near, 2), swap(far3, 6), swap(far2, 4)
    near_weights, near_dscore, local_k, local_v, mine, other = near_grads(
        queries, cotangent, exponent, dprob, final
    )
    near, far3, far2, other = together(near, far3, far2, other)
    keep, send = plane_sum(own, near, far2, far3)
    send, near_weights, c3a = together(send, near_weights, c3a)
    got = swap(send, 8)
    output, grad_queries = outputs(
        near_key, near_value, near_weights, near_dscore,
        mine_key, mine_value, mine_weights, mine_dscore,
        other_key, other_value, other_weights, other_dscore,
    )
    got, output = together(got, output)
    core = swap(other, 1)
    (c2,) = chip_sum(mine, core, ((64, BF16),))
    c2 = swap(c2, 2)
    c3a = swap(c3a, 4)
    keep = (keep + got[:16].astype(F32)).astype(BF16)
    two = swap(keep, 16)
    six = swap(jnp.where(rows_at(2, 2), keep, two), 56)
    parts = gather(local_k, local_v, core[:128], c2, c3a, far3, got[16:], two)
    six, *parts = together(six, *parts)
    grad_keys, grad_values = finish(*parts, six)
    return output, grad_queries, grad_keys, grad_values


def solution(mesh):
    spec = P(("dp", "ctx"), None)
    return jax.shard_map(
        per_device,
        mesh=mesh,
        in_specs=(spec,) * 4,
        out_specs=(spec,) * 4,
        check_vma=False,
    )
```

```python
import jax
import jax.numpy as jnp
from jax import lax
from jax.experimental import pallas as pl
from jax.experimental.pallas import tpu as pltpu
from jax.sharding import PartitionSpec as P

H = 8
DH = 128
D = H * DH
ROWS = 128
HALF_ROOT = 0.7071067811865476
SCALE = DH ** (-0.5)
LOG2E = 1.4426950408889634
F32 = jnp.float32
BF16 = jnp.bfloat16
VMEM_LIMIT = 16 * 1024 * 1024
PARAMS = pltpu.CompilerParams(vmem_limit_bytes=VMEM_LIMIT)


def swap(block, mask):
    count = lax.axis_size("ctx")
    return lax.ppermute(block, "ctx", [(i, i ^ mask) for i in range(count)])


def coarsen_kernel(
    k_hbm, v_hbm, q_hbm, g_hbm,
    c1_ref, c2_ref, c3_ref, c4_ref, c5_ref, c6_ref, k_ref, v_ref, q_ref, g_ref,
    tmp, pack, sems,
):
    def copy(source, target, number, columns):
        return pltpu.make_async_copy(
            source.at[:, columns], target.at[:, columns], sems.at[number]
        )

    half = D // 2
    sides = ((k_hbm, k_ref), (v_hbm, v_ref))
    copies = [
        copy(source, target, 2 * part + side, pl.ds(half * part, half))
        for part in range(2)
        for side, (source, target) in enumerate(sides)
    ]
    copies.append(copy(q_hbm, q_ref, 4, pl.ds(0, D)))
    copies.append(copy(g_hbm, g_ref, 5, pl.ds(0, D)))
    for each in copies:
        each.start()
    pack[...] = jnp.zeros(pack.shape, F32)
    for part in range(4):
        copies[part].wait()
        side = part % 2
        source = sides[side][1]
        for number in range(part // 2 * (H // 2), (part // 2 + 1) * (H // 2)):
            columns = slice(number * DH, number * DH + DH)
            plane = tmp.at[side * H + number]
            rows = source[:, columns].astype(F32)
            for level in range(1, 7):
                count = ROWS >> level
                plane[: 2 * count, :] = rows
                total = plane[pl.ds(0, count, stride=2), :] + plane[pl.ds(1, count, stride=2), :]
                exact = (total * HALF_ROOT).astype(BF16)
                rows = exact.astype(F32)
                if level < 4:
                    ref = (c1_ref, c2_ref, c3_ref)[level - 1]
                    ref[side * count : side * count + count, columns] = exact
                else:
                    for start in ((0,), (20,), (32, 34))[level - 4]:
                        start += 8 * side
                        pack[start : start + count, columns] = rows
    for number, ref in enumerate((c4_ref, c5_ref, c6_ref)):
        ref[...] = pack[16 * number : 16 * number + 16, :].astype(BF16)
    for each in copies[4:]:
        each.wait()


def coarsen(*operands):
    return pl.pallas_call(
        coarsen_kernel,
        out_shape=tuple(
            jax.ShapeDtypeStruct((count, D), BF16) for count in (128, 64, 32, 16, 16, 16) + (ROWS,) * 4
        ),
        in_specs=[pl.BlockSpec(memory_space=pltpu.HBM)] * 4,
        scratch_shapes=[
            pltpu.VMEM((2 * H, ROWS, DH), F32),
            pltpu.VMEM((48, D), F32),
            pltpu.SemaphoreType.DMA((6,)),
        ],
        compiler_params=PARAMS,
        name="coarsen",
    )(*operands)


def rows_at(first, count):
    row = lax.broadcasted_iota(jnp.int32, (16, 1), 0) % 8
    return (row >= first) & (row < first + count)


NEAR = 256
FAR = 128


def dot(a, b, a_dim, b_dim):
    return lax.dot_general(a, b, (((a_dim,), (b_dim,)), ((), ())), preferred_element_type=F32)


def by_head(body):
    def step(number, carry):
        body(pl.ds(pl.multiple_of(number * DH, DH), DH))
        return carry

    lax.fori_loop(0, H, step, 0, unroll=True)


def near_parts(c1, c2, c2_o):
    return (c1, 128, 64), (c2, 192, 32), (c2_o, 224, 32)


def near_kernel(q_ref, k_ref, v_ref, g_ref, *rest):
    parts, (key_ref, value_ref, exp_ref, dprob_ref, stats_ref) = rest[:3], rest[3:]
    key_ref[0:128, :] = k_ref[...]
    value_ref[0:128, :] = v_ref[...]
    for ref, start, count in near_parts(*parts):
        key_ref[start : start + count, :] = ref[:count, :]
        value_ref[start : start + count, :] = ref[count:, :]

    def head(columns):
        scores = dot(key_ref[:, columns], q_ref[:, columns], 1, 1)
        dprob = dot(value_ref[:, columns], g_ref[:, columns], 1, 1)
        top = jnp.max(scores, axis=0, keepdims=True)
        exponent = jnp.exp2((scores - top) * (SCALE * LOG2E))
        exp_ref[:, columns] = exponent
        dprob_ref[:, columns] = dprob
        stats_ref[0:1, columns] = top
        stats_ref[1:2, columns] = jnp.sum(exponent, axis=0, keepdims=True)
        stats_ref[2:3, columns] = jnp.sum(exponent * dprob, axis=0, keepdims=True)

    by_head(head)


def near_scores(*operands):
    shape = jax.ShapeDtypeStruct
    return pl.pallas_call(
        near_kernel,
        out_shape=(
            shape((NEAR, D), BF16),
            shape((NEAR, D), BF16),
            shape((NEAR, D), F32),
            shape((NEAR, D), F32),
            shape((8, D), F32),
        ),
        compiler_params=PARAMS,
        cost_estimate=pl.CostEstimate(
            flops=4 * NEAR * ROWS * D, bytes_accessed=8 * NEAR * D, transcendentals=NEAR * ROWS * H
        ),
        name="near_scores",
    )(*operands)


def place_far(tiles, key_ref, value_ref, key_tmp, value_tmp):
    for number, (ref, base) in enumerate(tiles):
        for tile in range(3):
            rows = ref[base + 16 * tile : base + 16 * tile + 16, :].astype(F32)
            start = 24 * number + 8 * tile
            key_tmp[start : start + 8, :] = rows[:8]
            value_tmp[start : start + 8, :] = rows[8:]
    key_ref[:96, :] = key_tmp[...].astype(BF16)
    value_ref[:96, :] = value_tmp[...].astype(BF16)
    for number, (ref, base) in enumerate(tiles[2:]):
        start = 96 + 16 * number
        key_ref[start : start + 16, :] = ref[base + 48 : base + 64, :]
        value_ref[start : start + 16, :] = ref[base + 64 : base + 80, :]


def pack_far(key_grad, value_grad, ref, columns):
    out = 0
    for number in range(4):
        pieces = [(24 * number + 8 * tile, 8) for tile in range(3)]
        if number > 1:
            pieces.append((96 + 16 * (number - 2), 16))
        for start, count in pieces:
            both = jnp.concatenate(
                [key_grad[start : start + count], value_grad[start : start + count]], axis=0
            )
            ref[out : out + 2 * count, columns] = both.astype(ref.dtype)
            out += 2 * count


def power(difference):
    return jnp.exp2(difference * (SCALE * LOG2E))


def mine_kernel(
    q_ref, g_ref, stats_ref, own, near, far2, far3,
    key_ref, value_ref, exp_ref, dprob_ref, joint_ref, key_tmp, value_tmp,
):
    tiles = ((own, 0), (near, 0), (far2, 0), (far3, 0))
    place_far(tiles, key_ref, value_ref, key_tmp, value_tmp)

    def head(columns):
        scores = dot(key_ref[:, columns], q_ref[:, columns], 1, 1)
        dprob = dot(value_ref[:, columns], g_ref[:, columns], 1, 1)
        old_top = stats_ref[0:1, columns]
        top = jnp.maximum(jnp.max(scores, axis=0, keepdims=True), old_top)
        exponent = power(scores - top)
        factor = power(old_top - top)
        exp_ref[:, columns] = exponent
        dprob_ref[:, columns] = dprob
        joint_ref[0:1, columns] = top
        joint_ref[1:2, columns] = factor * stats_ref[1:2, columns] + jnp.sum(
            exponent, axis=0, keepdims=True
        )
        joint_ref[2:3, columns] = factor * stats_ref[2:3, columns] + jnp.sum(
            exponent * dprob, axis=0, keepdims=True
        )
        joint_ref[3:4, columns] = factor

    by_head(head)


FAR_COST = pl.CostEstimate(
    flops=4 * FAR * ROWS * D, bytes_accessed=16 * FAR * D, transcendentals=FAR * ROWS * H
)
FAR_TMP = [pltpu.VMEM((96, D), F32), pltpu.VMEM((96, D), F32)]


def mine_scores(*operands):
    shape = jax.ShapeDtypeStruct
    return pl.pallas_call(
        mine_kernel,
        out_shape=(
            shape((FAR, D), BF16),
            shape((FAR, D), BF16),
            shape((FAR, D), F32),
            shape((FAR, D), F32),
            shape((8, D), F32),
        ),
        scratch_shapes=FAR_TMP,
        compiler_params=PARAMS,
        cost_estimate=FAR_COST,
        name="mine_scores",
    )(*operands)


def other_kernel(
    q_ref, g_ref, joint_ref, early, late,
    key_ref, value_ref, weight_ref, dscore_ref, final_ref, grad_ref,
    key_tmp, value_tmp, score_tmp, dprob_tmp,
):
    tiles = ((early, 0), (early, 48), (late, 0), (late, 80))
    place_far(tiles, key_ref, value_ref, key_tmp, value_tmp)

    def scores_of(columns):
        score_tmp[:, columns] = dot(key_ref[:, columns], q_ref[:, columns], 1, 1)
        dprob_tmp[:, columns] = dot(value_ref[:, columns], g_ref[:, columns], 1, 1)

    by_head(scores_of)
    old_top = joint_ref[0:1, :]
    top = jnp.maximum(jnp.max(score_tmp[...], axis=0, keepdims=True), old_top)
    factor = power(old_top - top)
    exponent = power(score_tmp[...] - top)
    dprob = dprob_tmp[...]
    total = factor * joint_ref[1:2, :] + jnp.sum(exponent, axis=0, keepdims=True)
    moment = factor * joint_ref[2:3, :] + jnp.sum(exponent * dprob, axis=0, keepdims=True)
    inverse = 1.0 / total
    delta = moment * inverse
    prob = exponent * inverse
    weight_ref[...] = prob.astype(BF16)
    dscore_ref[...] = (prob * (dprob - delta) * SCALE).astype(BF16)
    mine_factor = factor * inverse
    final_ref[0:1, :] = mine_factor * joint_ref[3:4, :]
    final_ref[1:2, :] = mine_factor
    final_ref[2:3, :] = delta

    def grads_of(columns):
        key_grad = dot(dscore_ref[:, columns], q_ref[:, columns], 1, 0)
        value_grad = dot(weight_ref[:, columns], g_ref[:, columns], 1, 0)
        pack_far(key_grad, value_grad, grad_ref, columns)

    by_head(grads_of)


def other_attend(*operands):
    shape = jax.ShapeDtypeStruct
    return pl.pallas_call(
        other_kernel,
        out_shape=(
            shape((FAR, D), BF16),
            shape((FAR, D), BF16),
            shape((FAR, D), BF16),
            shape((FAR, D), BF16),
            shape((8, D), F32),
            shape((2 * FAR, D), BF16),
        ),
        scratch_shapes=FAR_TMP + [pltpu.VMEM((FAR, D), F32), pltpu.VMEM((FAR, D), F32)],
        compiler_params=PARAMS,
        cost_estimate=FAR_COST,
        name="other_attend",
    )(*operands)


def soften(exp_ref, dprob_ref, final_ref, row, columns):
    prob = exp_ref[:, columns] * final_ref[row : row + 1, columns]
    dscore = prob * (dprob_ref[:, columns] - final_ref[2:3, columns]) * SCALE
    return prob.astype(BF16), dscore.astype(BF16)


def mine_grad_kernel(q_ref, g_ref, exp_ref, dprob_ref, final_ref, weight_ref, dscore_ref, grad_ref):
    def head(columns):
        weights, dscore = soften(exp_ref, dprob_ref, final_ref, 1, columns)
        weight_ref[:, columns] = weights
        dscore_ref[:, columns] = dscore
        key_grad = dot(dscore, q_ref[:, columns], 1, 0)
        pack_far(key_grad, dot(weights, g_ref[:, columns], 1, 0), grad_ref, columns)

    by_head(head)


def mine_grads(*operands):
    shape = jax.ShapeDtypeStruct
    return pl.pallas_call(
        mine_grad_kernel,
        out_shape=(shape((FAR, D), BF16), shape((FAR, D), BF16), shape((2 * FAR, D), F32)),
        compiler_params=PARAMS,
        cost_estimate=FAR_COST,
        name="mine_grads",
    )(*operands)


def near_grad_kernel(
    q_ref, g_ref, exp_ref, dprob_ref, final_ref,
    weight_ref, dscore_ref, local_k_ref, local_v_ref, mine_ref, other_ref,
):
    def head(columns):
        weights, dscore = soften(exp_ref, dprob_ref, final_ref, 0, columns)
        weight_ref[:, columns] = weights
        dscore_ref[:, columns] = dscore
        key_grad = dot(dscore, q_ref[:, columns], 1, 0)
        value_grad = dot(weights, g_ref[:, columns], 1, 0)
        local_k_ref[:, columns] = key_grad[0:128]
        local_v_ref[:, columns] = value_grad[0:128]
        targets = ((other_ref, 0), (mine_ref, 0), (other_ref, 128))
        for (ref, out), (_, start, count) in zip(targets, near_parts(*targets)):
            ref[out : out + count, columns] = key_grad[start : start + count].astype(ref.dtype)
            out += count
            ref[out : out + count, columns] = value_grad[start : start + count].astype(ref.dtype)

    by_head(head)


def near_grads(*operands):
    shape = jax.ShapeDtypeStruct
    return pl.pallas_call(
        near_grad_kernel,
        out_shape=(
            shape((NEAR, D), BF16),
            shape((NEAR, D), BF16),
            shape((ROWS, D), F32),
            shape((ROWS, D), F32),
            shape((64, D), F32),
            shape((192, D), BF16),
        ),
        compiler_params=PARAMS,
        cost_estimate=pl.CostEstimate(
            flops=4 * NEAR * ROWS * D, bytes_accessed=16 * NEAR * D, transcendentals=0
        ),
        name="near_grads",
    )(*operands)


def output_kernel(*refs):
    sets, (out_ref, grad_q_ref) = (refs[0:4], refs[4:8], refs[8:12]), refs[12:]

    def head(columns):
        output = grad_q = 0.0
        for key, value, weights, dscore in sets:
            output += dot(weights[:, columns], value[:, columns], 0, 0)
            grad_q += dot(dscore[:, columns], key[:, columns], 0, 0)
        out_ref[:, columns] = output.astype(BF16)
        grad_q_ref[:, columns] = grad_q.astype(BF16)

    by_head(head)


def outputs(*operands):
    shape = jax.ShapeDtypeStruct
    return pl.pallas_call(
        output_kernel,
        out_shape=(shape((ROWS, D), BF16), shape((ROWS, D), BF16)),
        compiler_params=PARAMS,
        cost_estimate=pl.CostEstimate(
            flops=8 * NEAR * ROWS * D, bytes_accessed=16 * NEAR * D, transcendentals=0
        ),
        name="outputs",
    )(*operands)


def chip_kernel(mine_ref, got_ref, *pieces):
    start = 0
    skip = got_ref.shape[0] - mine_ref.shape[0]
    for ref in pieces:
        count = ref.shape[0]
        got = got_ref[skip + start : skip + start + count, :].astype(F32)
        ref[...] = (mine_ref[start : start + count, :] + got).astype(ref.dtype)
        start += count


def chip_sum(mine, got, pieces):
    return pl.pallas_call(
        chip_kernel,
        out_shape=tuple(jax.ShapeDtypeStruct((count, D), kind) for count, kind in pieces),
        compiler_params=PARAMS,
        name="chip_sum",
    )(mine, got)


def plane_kernel(own_ref, near_ref, far2_ref, far3_ref, keep_ref, send_ref):
    total = (own_ref[...] + near_ref[...].astype(F32)) + (
        far2_ref[...].astype(F32) + far3_ref[:48, :].astype(F32)
    )
    keep_ref[...] = total[:16, :]
    send_ref[...] = total[16:, :].astype(BF16)


def plane_sum(own, near, far2, far3):
    return pl.pallas_call(
        plane_kernel,
        out_shape=(jax.ShapeDtypeStruct((16, D), F32), jax.ShapeDtypeStruct((32, D), BF16)),
        compiler_params=PARAMS,
        name="plane_sum",
    )(own, near, far2, far3)


def gather_kernel(
    local_k_ref, local_v_ref, c1_ref, c2_ref, c3_ref, far3_ref, z1_ref, z2_ref,
    grad_k_ref, grad_v_ref, tmp, pick,
):
    for number, ref in enumerate((z1_ref, z2_ref)):
        pick[16 * number : 16 * number + 16, :] = ref[...].astype(F32)
    for side, (local_ref, out_ref) in enumerate(
        ((local_k_ref, grad_k_ref), (local_v_ref, grad_v_ref))
    ):
        for number in range(H):
            columns = slice(number * DH, number * DH + DH)
            plane = tmp.at[side * H + number]

            def rows(ref, start, count, side=side, columns=columns):
                start += side * count
                return ref[start : start + count, columns].astype(F32)

            parts = {
                5: pick[20 + 8 * side : 24 + 8 * side, columns],
                4: rows(pick, 0, 8),
                3: rows(c3_ref, 0, 16) + rows(far3_ref, 48, 16),
                2: rows(c2_ref, 0, 32),
                1: rows(c1_ref, 0, 64),
                0: local_ref[:, columns],
            }
            total = parts[5]
            for level in range(4, -1, -1):
                count = ROWS >> level
                half = total * HALF_ROOT
                plane[pl.ds(0, count // 2, stride=2), :] = half
                plane[pl.ds(1, count // 2, stride=2), :] = half
                total = plane[:count, :] + parts[level]
            out_ref[:, columns] = total


def gather(*operands):
    shape = jax.ShapeDtypeStruct
    return pl.pallas_call(
        gather_kernel,
        out_shape=(shape((ROWS, D), F32), shape((ROWS, D), F32)),
        scratch_shapes=[pltpu.VMEM((2 * H, ROWS, DH), F32), pltpu.VMEM((32, D), F32)],
        compiler_params=PARAMS,
        cost_estimate=FAR_COST,
        name="gather",
    )(*operands)


def finish_kernel(part_k_ref, part_v_ref, z7_ref, grad_k_ref, grad_v_ref):
    top = z7_ref[...].astype(F32)
    for side, (part_ref, out_ref) in enumerate(
        ((part_k_ref, grad_k_ref), (part_v_ref, grad_v_ref))
    ):
        for row in range(2):
            first = 8 * side + row
            both = top[first : first + 1] + top[first + 2 : first + 3]
            rows = slice(64 * row, 64 * row + 64)
            out_ref[rows, :] = (part_ref[rows, :] + both * 0.125).astype(BF16)


def finish(*operands):
    shape = jax.ShapeDtypeStruct
    return pl.pallas_call(
        finish_kernel,
        out_shape=(shape((ROWS, D), BF16), shape((ROWS, D), BF16)),
        compiler_params=PARAMS,
        name="finish",
    )(*operands)


def together(*arrays):
    return lax.optimization_barrier(arrays)


def together(*arrays):
    return lax.optimization_barrier(arrays)


def per_device(queries, keys, values, cotangent):
    pinned = [
        pltpu.with_memory_space_constraint(array, pltpu.HBM)
        for array in (keys, values, queries, cotangent)
    ]
    c1, c2, c3, c4, c5, c6, keys, values, queries, cotangent = coarsen(*pinned)
    six = swap(c6, 56)
    c1 = swap(c1, 1)
    c2 = swap(c2, 2)
    c3a = swap(c3, 4)
    two = swap(jnp.where(rows_at(0, 2), six, c5), 16)
    keep = jnp.where(rows_at(2, 2), six, two)
    send, c2, c3a = together(jnp.concatenate([keep, c4]), c2, c3a)
    core = swap(c2, 1)
    own = jnp.concatenate([keep, swap(send, 8)])
    own, c1, c2, core = together(own, c1, c2, core)
    far = jnp.concatenate([own, c3])
    near, far3, far2 = swap(own, 2), swap(far, 6), swap(own, 4)
    near_key, near_value, exponent, dprob, stats = near_scores(
        queries, keys, values, cotangent, c1, c2, core
    )
    far2 = jnp.concatenate([far2, c3a])
    early = swap(jnp.concatenate([own, near]), 1)
    far3, stats = together(far3, stats)
    late = swap(jnp.concatenate([far2, far3]), 1)
    mine_key, mine_value, mine_exponent, mine_dprob, joint = mine_scores(
        queries, cotangent, stats, own, near, far2, far3
    )
    joint, *core = together(joint, early, late)
    other_key, other_value, other_weights, other_dscore, final, other = other_attend(
        queries, cotangent, joint, *core
    )
    got = swap(other, 1)
    mine_weights, mine_dscore, mine = mine_grads(
        queries, cotangent, mine_exponent, mine_dprob, final
    )
    got, mine = together(got, mine)
    own, near, far2, c3a, far3 = chip_sum(
        mine, got, ((48, F32), (48, BF16), (48, BF16), (32, BF16), (80, BF16))
    )
    final, near, far2, far3 = together(final, near, far2, far3)
    near, far3, far2 = swap(near, 2), swap(far3, 6), swap(far2, 4)
    near_weights, near_dscore, local_k, local_v, mine, other = near_grads(
        queries, cotangent, exponent, dprob, final
    )
    near, far3, far2, other = together(near, far3, far2, other)
    keep, send = plane_sum(own, near, far2, far3)
    send, near_weights, c3a = together(send, near_weights, c3a)
    got = swap(send, 8)
    output, grad_queries = outputs(
        near_key, near_value, near_weights, near_dscore,
        mine_key, mine_value, mine_weights, mine_dscore,
        other_key, other_value, other_weights, other_dscore,
    )
    got, output = together(got, output)
    core = swap(other, 1)
    (c2,) = chip_sum(mine, core, ((64, BF16),))
    c2 = swap(c2, 2)
    c3a = swap(c3a, 4)
    keep = (keep + got[:16].astype(F32)).astype(BF16)
    two = swap(keep, 16)
    six = swap(jnp.where(rows_at(2, 2), keep, two), 56)
    parts = gather(local_k, local_v, core[:128], c2, c3a, far3, got[16:], two)
    six, *parts = together(six, *parts)
    grad_keys, grad_values = finish(*parts, six)
    return output, grad_queries, grad_keys, grad_values


def solution(mesh):
    spec = P(("dp", "ctx"), None)
    return jax.shard_map(
        per_device,
        mesh=mesh,
        in_specs=(spec,) * 4,
        out_specs=(spec,) * 4,
        check_vma=False,
    )
```

```python
import jax
import jax.numpy as jnp
from jax import lax
from jax.experimental import pallas as pl
from jax.experimental.pallas import tpu as pltpu
from jax.sharding import PartitionSpec as P

H = 8
DH = 128
D = H * DH
ROWS = 128
HALF_ROOT = 0.7071067811865476
SCALE = DH ** (-0.5)
LOG2E = 1.4426950408889634
F32 = jnp.float32
BF16 = jnp.bfloat16
VMEM_LIMIT = 16 * 1024 * 1024
PARAMS = pltpu.CompilerParams(vmem_limit_bytes=VMEM_LIMIT)


def swap(block, mask):
    count = lax.axis_size("ctx")
    return lax.ppermute(block, "ctx", [(i, i ^ mask) for i in range(count)])


def coarsen_kernel(
    k_hbm, v_hbm, q_hbm, g_hbm,
    c1_ref, c2_ref, c3_ref, c4_ref, c5_ref, c6_ref, k_ref, v_ref, q_ref, g_ref,
    tmp, pack, sems,
):
    def copy(source, target, number, columns):
        return pltpu.make_async_copy(
            source.at[:, columns], target.at[:, columns], sems.at[number]
        )

    half = D // 2
    sides = ((k_hbm, k_ref), (v_hbm, v_ref))
    copies = [
        copy(source, target, 2 * part + side, pl.ds(half * part, half))
        for part in range(2)
        for side, (source, target) in enumerate(sides)
    ]
    copies.append(copy(q_hbm, q_ref, 4, pl.ds(0, D)))
    copies.append(copy(g_hbm, g_ref, 5, pl.ds(0, D)))
    for each in copies:
        each.start()
    pack[...] = jnp.zeros(pack.shape, F32)
    for part in range(4):
        copies[part].wait()
        side = part % 2
        source = sides[side][1]
        for number in range(part // 2 * (H // 2), (part // 2 + 1) * (H // 2)):
            columns = slice(number * DH, number * DH + DH)
            plane = tmp.at[side * H + number]
            rows = source[:, columns].astype(F32)
            for level in range(1, 7):
                count = ROWS >> level
                plane[: 2 * count, :] = rows
                total = plane[pl.ds(0, count, stride=2), :] + plane[pl.ds(1, count, stride=2), :]
                exact = (total * HALF_ROOT).astype(BF16)
                rows = exact.astype(F32)
                if level < 4:
                    ref = (c1_ref, c2_ref, c3_ref)[level - 1]
                    ref[side * count : side * count + count, columns] = exact
                else:
                    for start in ((0,), (20,), (32, 34))[level - 4]:
                        start += 8 * side
                        pack[start : start + count, columns] = rows
    for number, ref in enumerate((c4_ref, c5_ref, c6_ref)):
        ref[...] = pack[16 * number : 16 * number + 16, :].astype(BF16)
    for each in copies[4:]:
        each.wait()


def coarsen(*operands):
    return pl.pallas_call(
        coarsen_kernel,
        out_shape=tuple(
            jax.ShapeDtypeStruct((count, D), BF16) for count in (128, 64, 32, 16, 16, 16) + (ROWS,) * 4
        ),
        in_specs=[pl.BlockSpec(memory_space=pltpu.HBM)] * 4,
        scratch_shapes=[
            pltpu.VMEM((2 * H, ROWS, DH), F32),
            pltpu.VMEM((48, D), F32),
            pltpu.SemaphoreType.DMA((6,)),
        ],
        compiler_params=PARAMS,
        name="coarsen",
    )(*operands)


def rows_at(first, count):
    row = lax.broadcasted_iota(jnp.int32, (16, 1), 0) % 8
    return (row >= first) & (row < first + count)


NEAR = 256
FAR = 128


def dot(a, b, a_dim, b_dim):
    return lax.dot_general(a, b, (((a_dim,), (b_dim,)), ((), ())), preferred_element_type=F32)


def by_head(body):
    def step(number, carry):
        body(pl.ds(pl.multiple_of(number * DH, DH), DH))
        return carry

    lax.fori_loop(0, H, step, 0, unroll=True)


def near_parts(c1, c2, c2_o):
    return (c1, 128, 64), (c2, 192, 32), (c2_o, 224, 32)


def near_kernel(q_ref, k_ref, v_ref, g_ref, *rest):
    parts, (key_ref, value_ref, exp_ref, dprob_ref, stats_ref) = rest[:3], rest[3:]
    key_ref[0:128, :] = k_ref[...]
    value_ref[0:128, :] = v_ref[...]
    for ref, start, count in near_parts(*parts):
        key_ref[start : start + count, :] = ref[:count, :]
        value_ref[start : start + count, :] = ref[count:, :]

    def head(columns):
        scores = dot(key_ref[:, columns], q_ref[:, columns], 1, 1)
        dprob = dot(value_ref[:, columns], g_ref[:, columns], 1, 1)
        top = jnp.max(scores, axis=0, keepdims=True)
        exponent = jnp.exp2((scores - top) * (SCALE * LOG2E))
        exp_ref[:, columns] = exponent
        dprob_ref[:, columns] = dprob
        stats_ref[0:1, columns] = top
        stats_ref[1:2, columns] = jnp.sum(exponent, axis=0, keepdims=True)
        stats_ref[2:3, columns] = jnp.sum(exponent * dprob, axis=0, keepdims=True)

    by_head(head)


def near_scores(*operands):
    shape = jax.ShapeDtypeStruct
    return pl.pallas_call(
        near_kernel,
        out_shape=(
            shape((NEAR, D), BF16),
            shape((NEAR, D), BF16),
            shape((NEAR, D), F32),
            shape((NEAR, D), F32),
            shape((8, D), F32),
        ),
        compiler_params=PARAMS,
        cost_estimate=pl.CostEstimate(
            flops=4 * NEAR * ROWS * D, bytes_accessed=8 * NEAR * D, transcendentals=NEAR * ROWS * H
        ),
        name="near_scores",
    )(*operands)


def place_far(tiles, key_ref, value_ref, key_tmp, value_tmp):
    for number, (ref, base) in enumerate(tiles):
        for tile in range(3):
            rows = ref[base + 16 * tile : base + 16 * tile + 16, :].astype(F32)
            start = 24 * number + 8 * tile
            key_tmp[start : start + 8, :] = rows[:8]
            value_tmp[start : start + 8, :] = rows[8:]
    key_ref[:96, :] = key_tmp[...].astype(BF16)
    value_ref[:96, :] = value_tmp[...].astype(BF16)
    for number, (ref, base) in enumerate(tiles[2:]):
        start = 96 + 16 * number
        key_ref[start : start + 16, :] = ref[base + 48 : base + 64, :]
        value_ref[start : start + 16, :] = ref[base + 64 : base + 80, :]


def pack_far(key_grad, value_grad, ref, columns):
    out = 0
    for number in range(4):
        pieces = [(24 * number + 8 * tile, 8) for tile in range(3)]
        if number > 1:
            pieces.append((96 + 16 * (number - 2), 16))
        for start, count in pieces:
            both = jnp.concatenate(
                [key_grad[start : start + count], value_grad[start : start + count]], axis=0
            )
            ref[out : out + 2 * count, columns] = both.astype(ref.dtype)
            out += 2 * count


def power(difference):
    return jnp.exp2(difference * (SCALE * LOG2E))


def mine_kernel(
    q_ref, g_ref, stats_ref, own, near, far2, far3,
    key_ref, value_ref, exp_ref, dprob_ref, joint_ref, key_tmp, value_tmp,
):
    tiles = ((own, 0), (near, 0), (far2, 0), (far3, 0))
    place_far(tiles, key_ref, value_ref, key_tmp, value_tmp)

    def head(columns):
        scores = dot(key_ref[:, columns], q_ref[:, columns], 1, 1)
        dprob = dot(value_ref[:, columns], g_ref[:, columns], 1, 1)
        old_top = stats_ref[0:1, columns]
        top = jnp.maximum(jnp.max(scores, axis=0, keepdims=True), old_top)
        exponent = power(scores - top)
        factor = power(old_top - top)
        exp_ref[:, columns] = exponent
        dprob_ref[:, columns] = dprob
        joint_ref[0:1, columns] = top
        joint_ref[1:2, columns] = factor * stats_ref[1:2, columns] + jnp.sum(
            exponent, axis=0, keepdims=True
        )
        joint_ref[2:3, columns] = factor * stats_ref[2:3, columns] + jnp.sum(
            exponent * dprob, axis=0, keepdims=True
        )
        joint_ref[3:4, columns] = factor

    by_head(head)


FAR_COST = pl.CostEstimate(
    flops=4 * FAR * ROWS * D, bytes_accessed=16 * FAR * D, transcendentals=FAR * ROWS * H
)
FAR_TMP = [pltpu.VMEM((96, D), F32), pltpu.VMEM((96, D), F32)]


def mine_scores(*operands):
    shape = jax.ShapeDtypeStruct
    return pl.pallas_call(
        mine_kernel,
        out_shape=(
            shape((FAR, D), BF16),
            shape((FAR, D), BF16),
            shape((FAR, D), F32),
            shape((FAR, D), F32),
            shape((8, D), F32),
        ),
        scratch_shapes=FAR_TMP,
        compiler_params=PARAMS,
        cost_estimate=FAR_COST,
        name="mine_scores",
    )(*operands)


def other_kernel(
    q_ref, g_ref, joint_ref, early, late,
    key_ref, value_ref, weight_ref, dscore_ref, final_ref, grad_ref,
    key_tmp, value_tmp, score_tmp, dprob_tmp,
):
    tiles = ((early, 0), (late, 0), (late, 48), (late, 128))
    place_far(tiles, key_ref, value_ref, key_tmp, value_tmp)

    def scores_of(columns):
        score_tmp[:, columns] = dot(key_ref[:, columns], q_ref[:, columns], 1, 1)
        dprob_tmp[:, columns] = dot(value_ref[:, columns], g_ref[:, columns], 1, 1)

    by_head(scores_of)
    old_top = joint_ref[0:1, :]
    top = jnp.maximum(jnp.max(score_tmp[...], axis=0, keepdims=True), old_top)
    factor = power(old_top - top)
    exponent = power(score_tmp[...] - top)
    dprob = dprob_tmp[...]
    total = factor * joint_ref[1:2, :] + jnp.sum(exponent, axis=0, keepdims=True)
    moment = factor * joint_ref[2:3, :] + jnp.sum(exponent * dprob, axis=0, keepdims=True)
    inverse = 1.0 / total
    delta = moment * inverse
    prob = exponent * inverse
    weight_ref[...] = prob.astype(BF16)
    dscore_ref[...] = (prob * (dprob - delta) * SCALE).astype(BF16)
    mine_factor = factor * inverse
    final_ref[0:1, :] = mine_factor * joint_ref[3:4, :]
    final_ref[1:2, :] = mine_factor
    final_ref[2:3, :] = delta

    def grads_of(columns):
        key_grad = dot(dscore_ref[:, columns], q_ref[:, columns], 1, 0)
        value_grad = dot(weight_ref[:, columns], g_ref[:, columns], 1, 0)
        pack_far(key_grad, value_grad, grad_ref, columns)

    by_head(grads_of)


def other_attend(*operands):
    shape = jax.ShapeDtypeStruct
    return pl.pallas_call(
        other_kernel,
        out_shape=(
            shape((FAR, D), BF16),
            shape((FAR, D), BF16),
            shape((FAR, D), BF16),
            shape((FAR, D), BF16),
            shape((8, D), F32),
            shape((2 * FAR, D), BF16),
        ),
        scratch_shapes=FAR_TMP + [pltpu.VMEM((FAR, D), F32), pltpu.VMEM((FAR, D), F32)],
        compiler_params=PARAMS,
        cost_estimate=FAR_COST,
        name="other_attend",
    )(*operands)


def soften(exp_ref, dprob_ref, final_ref, row, columns):
    prob = exp_ref[:, columns] * final_ref[row : row + 1, columns]
    dscore = prob * (dprob_ref[:, columns] - final_ref[2:3, columns]) * SCALE
    return prob.astype(BF16), dscore.astype(BF16)


def mine_grad_kernel(q_ref, g_ref, exp_ref, dprob_ref, final_ref, weight_ref, dscore_ref, grad_ref):
    def head(columns):
        weights, dscore = soften(exp_ref, dprob_ref, final_ref, 1, columns)
        weight_ref[:, columns] = weights
        dscore_ref[:, columns] = dscore
        key_grad = dot(dscore, q_ref[:, columns], 1, 0)
        pack_far(key_grad, dot(weights, g_ref[:, columns], 1, 0), grad_ref, columns)

    by_head(head)


def mine_grads(*operands):
    shape = jax.ShapeDtypeStruct
    return pl.pallas_call(
        mine_grad_kernel,
        out_shape=(shape((FAR, D), BF16), shape((FAR, D), BF16), shape((2 * FAR, D), F32)),
        compiler_params=PARAMS,
        cost_estimate=FAR_COST,
        name="mine_grads",
    )(*operands)


def near_grad_kernel(
    q_ref, g_ref, exp_ref, dprob_ref, final_ref,
    weight_ref, dscore_ref, local_k_ref, local_v_ref, mine_ref, other_ref,
):
    def head(columns):
        weights, dscore = soften(exp_ref, dprob_ref, final_ref, 0, columns)
        weight_ref[:, columns] = weights
        dscore_ref[:, columns] = dscore
        key_grad = dot(dscore, q_ref[:, columns], 1, 0)
        value_grad = dot(weights, g_ref[:, columns], 1, 0)
        local_k_ref[:, columns] = key_grad[0:128]
        local_v_ref[:, columns] = value_grad[0:128]
        targets = ((other_ref, 0), (mine_ref, 0), (other_ref, 128))
        for (ref, out), (_, start, count) in zip(targets, near_parts(*targets)):
            ref[out : out + count, columns] = key_grad[start : start + count].astype(ref.dtype)
            out += count
            ref[out : out + count, columns] = value_grad[start : start + count].astype(ref.dtype)

    by_head(head)


def near_grads(*operands):
    shape = jax.ShapeDtypeStruct
    return pl.pallas_call(
        near_grad_kernel,
        out_shape=(
            shape((NEAR, D), BF16),
            shape((NEAR, D), BF16),
            shape((ROWS, D), F32),
            shape((ROWS, D), F32),
            shape((64, D), F32),
            shape((192, D), BF16),
        ),
        compiler_params=PARAMS,
        cost_estimate=pl.CostEstimate(
            flops=4 * NEAR * ROWS * D, bytes_accessed=16 * NEAR * D, transcendentals=0
        ),
        name="near_grads",
    )(*operands)


def output_kernel(*refs):
    sets, (out_ref, grad_q_ref) = (refs[0:4], refs[4:8], refs[8:12]), refs[12:]

    def head(columns):
        output = grad_q = 0.0
        for key, value, weights, dscore in sets:
            output += dot(weights[:, columns], value[:, columns], 0, 0)
            grad_q += dot(dscore[:, columns], key[:, columns], 0, 0)
        out_ref[:, columns] = output.astype(BF16)
        grad_q_ref[:, columns] = grad_q.astype(BF16)

    by_head(head)


def outputs(*operands):
    shape = jax.ShapeDtypeStruct
    return pl.pallas_call(
        output_kernel,
        out_shape=(shape((ROWS, D), BF16), shape((ROWS, D), BF16)),
        compiler_params=PARAMS,
        cost_estimate=pl.CostEstimate(
            flops=8 * NEAR * ROWS * D, bytes_accessed=16 * NEAR * D, transcendentals=0
        ),
        name="outputs",
    )(*operands)


def chip_kernel(mine_ref, got_ref, *pieces):
    start = 0
    skip = got_ref.shape[0] - mine_ref.shape[0]
    for ref in pieces:
        count = ref.shape[0]
        got = got_ref[skip + start : skip + start + count, :].astype(F32)
        ref[...] = (mine_ref[start : start + count, :] + got).astype(ref.dtype)
        start += count


def chip_sum(mine, got, pieces):
    return pl.pallas_call(
        chip_kernel,
        out_shape=tuple(jax.ShapeDtypeStruct((count, D), kind) for count, kind in pieces),
        compiler_params=PARAMS,
        name="chip_sum",
    )(mine, got)


def plane_kernel(own_ref, near_ref, far2_ref, far3_ref, keep_ref, send_ref):
    total = (own_ref[...] + near_ref[...].astype(F32)) + (
        far2_ref[...].astype(F32) + far3_ref[:48, :].astype(F32)
    )
    keep_ref[...] = total[:16, :]
    send_ref[...] = total[16:, :].astype(BF16)


def plane_sum(own, near, far2, far3):
    return pl.pallas_call(
        plane_kernel,
        out_shape=(jax.ShapeDtypeStruct((16, D), F32), jax.ShapeDtypeStruct((32, D), BF16)),
        compiler_params=PARAMS,
        name="plane_sum",
    )(own, near, far2, far3)


def gather_kernel(
    local_k_ref, local_v_ref, c1_ref, c2_ref, c3_ref, far3_ref, z1_ref, z2_ref,
    grad_k_ref, grad_v_ref, tmp, pick,
):
    for number, ref in enumerate((z1_ref, z2_ref)):
        pick[16 * number : 16 * number + 16, :] = ref[...].astype(F32)
    for side, (local_ref, out_ref) in enumerate(
        ((local_k_ref, grad_k_ref), (local_v_ref, grad_v_ref))
    ):
        for number in range(H):
            columns = slice(number * DH, number * DH + DH)
            plane = tmp.at[side * H + number]

            def rows(ref, start, count, side=side, columns=columns):
                start += side * count
                return ref[start : start + count, columns].astype(F32)

            parts = {
                5: pick[20 + 8 * side : 24 + 8 * side, columns],
                4: rows(pick, 0, 8),
                3: rows(c3_ref, 0, 16) + rows(far3_ref, 48, 16),
                2: rows(c2_ref, 0, 32),
                1: rows(c1_ref, 0, 64),
                0: local_ref[:, columns],
            }
            total = parts[5]
            for level in range(4, -1, -1):
                count = ROWS >> level
                half = total * HALF_ROOT
                plane[pl.ds(0, count // 2, stride=2), :] = half
                plane[pl.ds(1, count // 2, stride=2), :] = half
                total = plane[:count, :] + parts[level]
            out_ref[:, columns] = total


def gather(*operands):
    shape = jax.ShapeDtypeStruct
    return pl.pallas_call(
        gather_kernel,
        out_shape=(shape((ROWS, D), F32), shape((ROWS, D), F32)),
        scratch_shapes=[pltpu.VMEM((2 * H, ROWS, DH), F32), pltpu.VMEM((32, D), F32)],
        compiler_params=PARAMS,
        cost_estimate=FAR_COST,
        name="gather",
    )(*operands)


def finish_kernel(part_k_ref, part_v_ref, z7_ref, grad_k_ref, grad_v_ref):
    top = z7_ref[...].astype(F32)
    for side, (part_ref, out_ref) in enumerate(
        ((part_k_ref, grad_k_ref), (part_v_ref, grad_v_ref))
    ):
        for row in range(2):
            first = 8 * side + row
            both = top[first : first + 1] + top[first + 2 : first + 3]
            rows = slice(64 * row, 64 * row + 64)
            out_ref[rows, :] = (part_ref[rows, :] + both * 0.125).astype(BF16)


def finish(*operands):
    shape = jax.ShapeDtypeStruct
    return pl.pallas_call(
        finish_kernel,
        out_shape=(shape((ROWS, D), BF16), shape((ROWS, D), BF16)),
        compiler_params=PARAMS,
        name="finish",
    )(*operands)


def together(*arrays):
    return lax.optimization_barrier(arrays)


def together(*arrays):
    return lax.optimization_barrier(arrays)


def per_device(queries, keys, values, cotangent):
    pinned = [
        pltpu.with_memory_space_constraint(array, pltpu.HBM)
        for array in (keys, values, queries, cotangent)
    ]
    c1, c2, c3, c4, c5, c6, keys, values, queries, cotangent = coarsen(*pinned)
    six = swap(c6, 56)
    c1 = swap(c1, 1)
    c2 = swap(c2, 2)
    c3a = swap(c3, 4)
    two = swap(jnp.where(rows_at(0, 2), six, c5), 16)
    keep = jnp.where(rows_at(2, 2), six, two)
    send, c2, c3a = together(jnp.concatenate([keep, c4]), c2, c3a)
    core = swap(c2, 1)
    own = jnp.concatenate([keep, swap(send, 8)])
    own, c1, c2, core = together(own, c1, c2, core)
    far = jnp.concatenate([own, c3])
    near, far3, far2 = swap(own, 2), swap(far, 6), swap(own, 4)
    near_key, near_value, exponent, dprob, stats = near_scores(
        queries, keys, values, cotangent, c1, c2, core
    )
    far2 = jnp.concatenate([far2, c3a])
    early = swap(own, 1)
    far3, stats = together(far3, stats)
    late = swap(jnp.concatenate([near, far2, far3]), 1)
    mine_key, mine_value, mine_exponent, mine_dprob, joint = mine_scores(
        queries, cotangent, stats, own, near, far2, far3
    )
    joint, *core = together(joint, early, late)
    other_key, other_value, other_weights, other_dscore, final, other = other_attend(
        queries, cotangent, joint, *core
    )
    got = swap(other, 1)
    mine_weights, mine_dscore, mine = mine_grads(
        queries, cotangent, mine_exponent, mine_dprob, final
    )
    got, mine = together(got, mine)
    own, near, far2, c3a, far3 = chip_sum(
        mine, got, ((48, F32), (48, BF16), (48, BF16), (32, BF16), (80, BF16))
    )
    final, near, far2, far3 = together(final, near, far2, far3)
    near, far3, far2 = swap(near, 2), swap(far3, 6), swap(far2, 4)
    near_weights, near_dscore, local_k, local_v, mine, other = near_grads(
        queries, cotangent, exponent, dprob, final
    )
    near, far3, far2, other = together(near, far3, far2, other)
    keep, send = plane_sum(own, near, far2, far3)
    send, near_weights, c3a = together(send, near_weights, c3a)
    got = swap(send, 8)
    output, grad_queries = outputs(
        near_key, near_value, near_weights, near_dscore,
        mine_key, mine_value, mine_weights, mine_dscore,
        other_key, other_value, other_weights, other_dscore,
    )
    got, output = together(got, output)
    core = swap(other, 1)
    (c2,) = chip_sum(mine, core, ((64, BF16),))
    c2 = swap(c2, 2)
    c3a = swap(c3a, 4)
    keep = (keep + got[:16].astype(F32)).astype(BF16)
    two = swap(keep, 16)
    six = swap(jnp.where(rows_at(2, 2), keep, two), 56)
    parts = gather(local_k, local_v, core[:128], c2, c3a, far3, got[16:], two)
    six, *parts = together(six, *parts)
    grad_keys, grad_values = finish(*parts, six)
    return output, grad_queries, grad_keys, grad_values


def solution(mesh):
    spec = P(("dp", "ctx"), None)
    return jax.shard_map(
        per_device,
        mesh=mesh,
        in_specs=(spec,) * 4,
        out_specs=(spec,) * 4,
        check_vma=False,
    )
```
